256 devices in a mesh: tm: 8 (over z), atom: 2 (over x_lo), chan: 16 (over y, x_hi, core).
Axes of the slice: x: 4 (x_hi: 2, x_lo: 2; x = x_hi * 2 + x_lo), y: 4, z: 8, core: 2. Of those that a mesh axis runs over, the one named last changes fastest.
Arguments:
- signal: bfloat16 [256, 8192], P('chan', 'tm'), may hold values from -6 to 6
- codes_init: float32 [128, 8192], P('atom', 'tm'), may hold values from -4 to 4
- atom_bank: bfloat16 [128, 256, 512], P('atom', 'chan'), may hold values from -0.015625 to 0.015625
- step_size: float32 [128], P('atom'), may hold values from 0.1 to 0.5
- threshold: float32 [128], P('atom'), may hold values from 0.3 to 3
Outputs:
- final_codes: float32 [128, 8192], P('atom', 'tm')
- residual: float32 [256, 8192], P('chan', 'tm')
The draws below stay inside these ranges and needn't reach their ends.
All inputs are finite; a program needn't handle non-finite values.
Results may differ from the reference program's by a relative error of at most 0.0025.
Values may be sent and summed in bfloat16 or wider, within the bound.
A program may use at most 64 MiB of HBM per device.

```python
import math
import jax
import jax.numpy as jnp
from jax import lax

ATOMS = 128
CHANNELS = 256
TAPS = 512
ITERS = 2
SAMPLES = 8192


def block_levels(stream_key, extent, shards, least, top_value):
    gain, own = 1.0, jax.random.fold_in(stream_key, 6)
    for position, parts in shards:
        steps = jnp.exp(jax.random.uniform(jax.random.fold_in(own, position), (parts,), jnp.float32, least / len(shards), top_value / len(shards)))
        gain = gain * jnp.repeat(steps, extent[position] // parts).reshape([-1 if axis == position else 1 for axis in range(len(extent))])
    return gain


def normal_values(rng, shape, width, limit, split=(), held_as=jnp.bfloat16):
    loudness = block_levels(rng, shape, split, -0.22, 0.18) if split else 1.0
    array = jax.random.normal(rng, shape, jnp.float32) * width * loudness
    return jnp.minimum(jnp.maximum(array, -limit), limit).astype(held_as)


def setup_inputs(seed: int = 0) -> dict:
    splits = jax.random.split(jax.random.key(seed), 6)
    return {
        "signal": normal_values(splits[0], (CHANNELS, SAMPLES), 1.0, 6.0, ((0, 16), (1, 8))),
        "codes_init": normal_values(splits[1], (ATOMS, SAMPLES), 0.5, 4.0, ((0, 2), (1, 8)), jnp.float32),
        "atom_bank": normal_values(splits[2], (ATOMS, CHANNELS, TAPS), (CHANNELS * TAPS) ** -0.5, 0.015625, ((0, 2), (1, 16))),
        "step_size": jnp.clip(jnp.exp(math.log(0.5) - 1.609438 * jax.random.uniform(splits[3], (ATOMS,), jnp.float32) ** block_levels(splits[3], (ATOMS,), ((0, 2),), -0.2, 0.2)), 0.1, 0.5),
        "threshold": jnp.clip(jnp.exp(math.log(3.0) - 2.3025851 * jax.random.uniform(splits[4], (ATOMS,), jnp.float32) ** block_levels(splits[4], (ATOMS,), ((0, 2),), -0.2, 0.2)), 0.3, 3.0),
    }


def convolve(extended, kernel, spec):
    return lax.conv_general_dilated(extended[None], kernel, (1,), "VALID", dimension_numbers=("NCH", spec, "NCH"), precision=lax.Precision.HIGHEST)[0]


def shrink(current, gradient, step_size, threshold):
    moved = current - step_size[:, None] * gradient
    bound = (step_size * threshold)[:, None]
    return moved - jnp.clip(moved, -bound, bound)


def reference(signal, codes_init, atom_bank, step_size, threshold):
    kernel = atom_bank.astype(jnp.float32)
    flipped = kernel[:, :, ::-1]
    current = codes_init
    misfit = None
    for sweep_index in range(ITERS):
        lowered = current.astype(jnp.bfloat16).astype(jnp.float32)
        padded = jnp.pad(lowered, ((0, 0), (TAPS - 1, 0)))
        recon = convolve(padded, flipped, "IOH")
        misfit = recon - signal.astype(jnp.float32)
        rounded = misfit.astype(jnp.bfloat16)
        trailing = jnp.pad(rounded.astype(jnp.float32), ((0, 0), (0, TAPS - 1)))
        gradient = convolve(trailing, kernel, "OIH")
        current = shrink(current, gradient, step_size, threshold)
    return current, misfit
```

```python
import functools

import jax
import jax.numpy as jnp
from jax import lax
from jax.experimental import pallas as pl
from jax.experimental.pallas import tpu as pltpu
from jax.sharding import PartitionSpec as P

F32, BF16 = jnp.float32, jnp.bfloat16
MESH = pl.DeviceIdType.MESH
ITERS = 2
ATOMS, CHANS, TAPS, SLAB = 64, 16, 512, 1024
LANES, HALF = 128, 512
GROUP = 16


def tile_iota(rows, columns, dimension):
    return lax.broadcasted_iota(jnp.int32, (rows, columns), dimension)


def matmul(left, right):
    return jnp.dot(left, right, preferred_element_type=F32)


def arrange_bank(bank, natural, synthesis, gradient):
    row, column = tile_iota(256, 256, 0), tile_iota(256, 256, 1)
    swap = ((row // 16 == column % 16) & (row % 16 == column // 16)).astype(BF16)
    for part in range(4):
        swapped = matmul(swap, bank[256 * part : 256 * part + 256, :]).astype(BF16)
        for c in range(CHANS):
            for h in range(4):
                natural[64 * h + 16 * part : 64 * h + 16 * part + 16, 128 * c : 128 * c + 128] = (
                    swapped[16 * c : 16 * c + 16, 128 * h : 128 * h + 128]
                )
    eye = (tile_iota(128, 128, 0) == tile_iota(128, 128, 1)).astype(BF16)
    for c in range(CHANS):
        turned = lax.dot_general(
            eye,
            natural[:, 128 * c : 128 * c + 128],
            (((1,), (1,)), ((), ())),
            preferred_element_type=F32,
        ).astype(BF16)
        for j in range(8):
            synthesis[16 * c : 16 * c + 16, 256 * j : 256 * j + 256] = turned[16 * j : 16 * j + 16, :]
    row, column = tile_iota(512, 512, 0), tile_iota(512, 512, 1)
    select = (
        (row // 128 == column // 32 % 4)
        & (row // 32 % 4 == column // 128)
        & (row % 32 == 31 - column % 32)
    ).astype(BF16)
    for cg in range(4):
        moved = matmul(natural[:, 512 * cg : 512 * cg + 512], select).astype(BF16)
        for h in range(4):
            for q in range(4):
                at = 128 * (4 * cg + h)
                gradient[64 * q : 64 * q + 64, at : at + 128] = moved[
                    64 * h : 64 * h + 64, 128 * q : 128 * q + 128
                ]


def shift_codes(codes, keep, shifted, place):
    width = codes.shape[1]
    for j in range(8):
        shifted[j, :, place : place + keep] = pltpu.roll(codes, width - (113 - 16 * j), 1)[:, :keep]


def synthesize(shifted, synthesis, spread, begin, end):
    for start in range(begin, end, 256):
        stop = min(start + 256, end)
        total = None
        for j in range(8):
            window = jnp.concatenate(
                [shifted[j, :, start - 128 * h + 384 : stop - 128 * h + 384] for h in range(4)], axis=0
            )
            part = matmul(synthesis[:, 256 * j : 256 * j + 256], window)
            total = part if total is None else total + part
        spread[:, start:stop] = total


def gather_rows(spread, begin):
    rows = []
    for c in range(CHANS):
        low = spread[16 * c : 16 * c + 8, begin : begin + 640]
        high = spread[16 * c + 8 : 16 * c + 16, begin : begin + 640]
        both = pltpu.roll(low, 640 - 15, 1, stride=1, stride_axis=0) + pltpu.roll(
            high, 640 - 7, 1, stride=1, stride_axis=0
        )
        rows.append(jnp.sum(both[:, :HALF], axis=0, keepdims=True))
    return jnp.concatenate(rows, axis=0)


def shift_misfit(misfit, first, last, drop, shifted):
    begin, end = 128 * (first + drop), 128 * last
    for c in range(CHANS):
        row = jnp.broadcast_to(misfit[c : c + 1, 128 * first : end], (16, end - 128 * first)).astype(BF16)
        near = pltpu.roll(row, 1, 1, stride=1, stride_axis=0)
        far = pltpu.roll(near, 16, 1)
        at = 32 * (c % 4)
        shifted[c // 4, at : at + 16, begin:end] = near[:, 128 * drop :]
        shifted[c // 4, at + 16 : at + 32, begin:end] = far[:, 128 * drop :]


def correlate(shifted, gradient, spread, begin, end):
    for start in range(begin, end, 256):
        stop = min(start + 256, end)
        total = None
        for cg in range(4):
            for h in (0, 2):
                window = jnp.concatenate(
                    [
                        shifted[cg, :, start + 128 * h : stop + 128 * h],
                        shifted[cg, :, start + 128 * h + 128 : stop + 128 * h + 128],
                    ],
                    axis=0,
                )
                at = 128 * (4 * cg + h)
                part = matmul(gradient[:, at : at + 256], window)
                total = part if total is None else total + part
        spread[:, start:stop] = total


def gather_taps(spread, begin):
    total = spread[192:256, begin + 128 : begin + 640]
    for q in range(3):
        rows = spread[64 * q : 64 * q + 64, begin : begin + 640]
        total = total + pltpu.roll(rows, 96 - 32 * q, 1)[:, 128:]
    return total


def column_of(row):
    diagonal = tile_iota(ATOMS, ATOMS, 0) == tile_iota(ATOMS, ATOMS, 1)
    return jnp.sum(jnp.where(diagonal, jnp.broadcast_to(row, (ATOMS, ATOMS)), 0.0), axis=1, keepdims=True)


def kernel(
    slabs,
    bank,
    codes,
    signal,
    step_size,
    threshold,
    out_codes,
    out_residual,
    natural,
    synthesis,
    gradient,
    lowered,
    own,
    code_shift,
    spread,
    part,
    from_atom,
    from_next,
    misfit,
    misfit_shift,
    grad_send,
    grad_recv,
    code_send,
    scales,
    halo_sems,
    part_send,
    part_recv,
    grad_send_sem,
    grad_recv_sem,
    code_send_sem,
    code_recv_sem,
    edge_send_sem,
    edge_recv_sem,
):
    tm, atom, me = lax.axis_index("tm"), lax.axis_index("atom"), lax.axis_index("chan")
    after, before = lax.rem(tm + 1, slabs), lax.rem(tm + slabs - 1, slabs)
    other = 1 - atom
    my_rows = pl.multiple_of(me // 4 * 16, 16)
    my_block = lax.rem(me, 4)

    barrier = pltpu.get_barrier_semaphore()

    def greet(device):
        pl.semaphore_signal(barrier, 1, device_id=device, device_id_type=MESH)

    def greet_group(turn, carry):
        greet({"chan": lax.rem(me + turn, GROUP)})
        return carry

    def greet_before(turn, carry):
        greet({"tm": before, "chan": lax.rem(me + turn, GROUP)})
        return carry

    greet({"atom": other})
    greet({"tm": after})
    greet({"tm": after, "atom": other})
    lax.fori_loop(0, GROUP, greet_before, 0)
    lax.fori_loop(1, GROUP, greet_group, 0)

    for block in range(8):
        lowered[1 + block // 4, block % 4] = codes[:, 128 * block : 128 * block + 128].astype(BF16)
    arrange_bank(bank, natural, synthesis, gradient)
    scales[:, 0:1] = column_of(step_size[...])
    scales[:, 1:2] = column_of(threshold[...])
    for half in range(2):
        at = pl.multiple_of((my_block + 4 * half) * 128, 128)
        own[half] = codes[pl.ds(my_rows, 16), pl.ds(at, 128)]

    def codes_of(first, last):
        return jnp.concatenate([lowered[b // 4, b % 4] for b in range(first, last)], axis=1)

    def late_half(sweep):
        shift_codes(codes_of(4, 12), 1024, code_shift, 512)
        synthesize(code_shift, synthesis, spread, 512, 1152)
        recon = gather_rows(spread, 512)
        part[sweep, 1] = recon - jnp.where(atom == 0, signal[:, HALF:].astype(F32), 0.0)

    def early_half(sweep):
        edge = jnp.where(tm > 0, codes_of(0, 4).astype(F32), 0.0).astype(BF16)
        shift_codes(jnp.concatenate([edge, lowered[1, 0]], axis=1), 512, code_shift, 0)
        synthesize(code_shift, synthesis, spread, 0, 512)
        recon = gather_rows(spread, 0)
        part[sweep, 0] = recon - jnp.where(atom == 0, signal[:, :HALF].astype(F32), 0.0)

    def part_copy(sweep, index, half, target, device):
        return pltpu.make_async_remote_copy(
            src_ref=part.at[sweep, half],
            dst_ref=target,
            send_sem=part_send.at[sweep, index],
            recv_sem=part_recv.at[sweep, index],
            device_id=device,
            device_id_type=MESH,
        )

    def grad_copy(half, turn):
        owner = lax.rem(me + turn, GROUP)
        return pltpu.make_async_remote_copy(
            src_ref=grad_send.at[half, owner],
            dst_ref=grad_recv.at[half, turn],
            send_sem=grad_send_sem.at[half, turn],
            recv_sem=grad_recv_sem.at[half, turn],
            device_id={"chan": owner},
            device_id_type=MESH,
        )

    def code_place(last, half):
        if last:
            at = pl.multiple_of((my_block + 4 * half) * 128, 128)
            return out_codes.at[pl.ds(my_rows, 16), pl.ds(at, 128)]
        return lowered.at[1 + half, my_block, pl.ds(my_rows, 16)]

    def code_copy(last, half, turn):
        return pltpu.make_async_remote_copy(
            src_ref=own.at[half] if last else code_send.at[half],
            dst_ref=code_place(last, half),
            send_sem=code_send_sem.at[half, turn],
            recv_sem=code_recv_sem.at[half, turn],
            device_id={"chan": lax.rem(me + turn, GROUP)},
            device_id_type=MESH,
        )

    def edge_copy(turn):
        return pltpu.make_async_remote_copy(
            src_ref=code_send.at[1],
            dst_ref=lowered.at[0, my_block, pl.ds(my_rows, 16)],
            send_sem=edge_send_sem.at[turn],
            recv_sem=edge_recv_sem.at[turn],
            device_id={"tm": after, "chan": lax.rem(me + turn, GROUP)},
            device_id_type=MESH,
        )

    def each(first, act):
        def run(turn, carry):
            act(turn)
            return carry

        lax.fori_loop(first, GROUP, run, 0)

    halo = pltpu.make_async_remote_copy(
        src_ref=lowered.at[2],
        dst_ref=lowered.at[0],
        send_sem=halo_sems.at[0],
        recv_sem=halo_sems.at[1],
        device_id={"tm": after},
        device_id_type=MESH,
    )

    for sweep in range(ITERS):
        last = sweep == ITERS - 1
        copies = [
            part_copy(sweep, 0, 1, from_atom.at[sweep, 1], {"atom": other}),
            part_copy(sweep, 1, 0, from_atom.at[sweep, 0], {"atom": other}),
            part_copy(sweep, 2, 0, from_next.at[sweep, 0], {"tm": before}),
            part_copy(sweep, 3, 0, from_next.at[sweep, 1], {"tm": before, "atom": other}),
        ]
        late_half(sweep)
        if sweep == 0:
            pl.semaphore_wait(barrier, 2 * GROUP + 2)
            halo.start()
        copies[0].start()
        if sweep == 0:
            halo.wait()
        else:
            each(0, lambda turn: edge_copy(turn).wait())
        early_half(sweep)
        for copy in (copies[3], copies[2], copies[1]):
            copy.start()

        copies[0].wait_recv()
        whole = part[sweep, 1] + from_atom[sweep, 1]
        misfit[:, HALF:SLAB] = whole
        if last:
            out_residual[:, HALF:SLAB] = whole
        shift_misfit(misfit, 4, 8, 1, misfit_shift)
        copies[1].wait_recv()
        whole = part[sweep, 0] + from_atom[sweep, 0]
        misfit[:, :HALF] = whole
        if last:
            out_residual[:, :HALF] = whole
        shift_misfit(misfit, 0, 5, 0, misfit_shift)
        correlate(misfit_shift, gradient, spread, 0, 640)

        def put(half):
            total = gather_taps(spread, HALF * half)
            for owner in range(GROUP):
                row, block = owner // 4 * 16, owner % 4 * 128
                grad_send[half, owner] = total[row : row + 16, block : block + 128]
            each(1, lambda turn: grad_copy(half, turn).start())

        put(0)
        copies[2].wait_recv()
        copies[3].wait_recv()
        whole = from_next[sweep, 0] + from_next[sweep, 1]
        misfit[:, SLAB:] = jnp.where(tm < slabs - 1, whole, 0.0)
        shift_misfit(misfit, 7, 12, 1, misfit_shift)
        correlate(misfit_shift, gradient, spread, 640, 1152)
        put(1)

        for half in range(2):
            each(1, lambda turn: grad_copy(half, turn).wait_recv())
            total = grad_send[half, me]
            for turn in range(1, GROUP):
                total = total + grad_recv[half, turn]
            step = scales[pl.ds(my_rows, 16), 0:1]
            bound = step * scales[pl.ds(my_rows, 16), 1:2]
            moved = own[half] - step * total
            updated = moved - jnp.clip(moved, -bound, bound)
            own[half] = updated
            if not last:
                code_send[half] = updated.astype(BF16)
            each(1, lambda turn: code_copy(last, half, turn).start())
            if half == 1 and not last:
                each(0, lambda turn: edge_copy(turn).start())
            code_place(last, half)[...] = updated if last else updated.astype(BF16)
        for half in range(2):
            each(1, lambda turn: code_copy(last, half, turn).wait())
            each(1, lambda turn: grad_copy(half, turn).wait_send())
        for copy in copies:
            copy.wait_send()


def body(signal, codes_init, atom_bank, step_size, threshold):
    vmem = pl.BlockSpec(memory_space=pltpu.VMEM)
    return pl.pallas_call(
        functools.partial(kernel, lax.axis_size("tm")),
        out_shape=(
            jax.ShapeDtypeStruct((ATOMS, SLAB), F32),
            jax.ShapeDtypeStruct((CHANS, SLAB), F32),
        ),
        in_specs=[vmem] * 5,
        out_specs=(vmem, vmem),
        scratch_shapes=[
            pltpu.VMEM((256, 2048), BF16),
            pltpu.VMEM((256, 2048), BF16),
            pltpu.VMEM((256, 2048), BF16),
            pltpu.VMEM((3, 4, ATOMS, LANES), BF16),
            pltpu.VMEM((2, 16, LANES), F32),
            pltpu.VMEM((8, ATOMS, 1536), BF16),
            pltpu.VMEM((256, 1152), F32),
            pltpu.VMEM((ITERS, 2, CHANS, HALF), F32),
            pltpu.VMEM((ITERS, 2, CHANS, HALF), F32),
            pltpu.VMEM((ITERS, 2, CHANS, HALF), F32),
            pltpu.VMEM((CHANS, 1536), F32),
            pltpu.VMEM((4, 128, 1536), BF16),
            pltpu.VMEM((2, GROUP, 16, LANES), F32),
            pltpu.VMEM((2, GROUP, 16, LANES), F32),
            pltpu.VMEM((2, 16, LANES), BF16),
            pltpu.VMEM((ATOMS, LANES), F32),
            pltpu.SemaphoreType.DMA((2,)),
            pltpu.SemaphoreType.DMA((ITERS, 4)),
            pltpu.SemaphoreType.DMA((ITERS, 4)),
            pltpu.SemaphoreType.DMA((2, GROUP)),
            pltpu.SemaphoreType.DMA((2, GROUP)),
            pltpu.SemaphoreType.DMA((2, GROUP)),
            pltpu.SemaphoreType.DMA((2, GROUP)),
            pltpu.SemaphoreType.DMA((GROUP,)),
            pltpu.SemaphoreType.DMA((GROUP,)),
        ],
        compiler_params=pltpu.CompilerParams(
            collective_id=0, has_side_effects=True, vmem_limit_bytes=48 * 1024 * 1024
        ),
    )(
        atom_bank.reshape(ATOMS * CHANS, TAPS),
        codes_init,
        signal,
        step_size.reshape(1, ATOMS),
        threshold.reshape(1, ATOMS),
    )


def solution(mesh):
    placed = (P("chan", "tm"), P("atom", "tm"), P("atom", "chan", None), P("atom"), P("atom"))
    return jax.shard_map(
        body,
        mesh=mesh,
        in_specs=placed,
        out_specs=(P("atom", "tm"), P("chan", "tm")),
        check_vma=False,
    )
```

```python
import functools

import jax
import jax.numpy as jnp
from jax import lax
from jax.experimental import pallas as pl
from jax.experimental.pallas import tpu as pltpu
from jax.sharding import PartitionSpec as P

F32, BF16 = jnp.float32, jnp.bfloat16
MESH = pl.DeviceIdType.MESH
ITERS = 2
ATOMS, CHANS, TAPS, SLAB = 64, 16, 512, 1024
LANES, HALF = 128, 512
GROUP = 16


def tile_iota(rows, columns, dimension):
    return lax.broadcasted_iota(jnp.int32, (rows, columns), dimension)


def matmul(left, right):
    return jnp.dot(left, right, preferred_element_type=F32)


def arrange_bank(bank, natural, synthesis, gradient):
    row, column = tile_iota(256, 256, 0), tile_iota(256, 256, 1)
    swap = ((row // 16 == column % 16) & (row % 16 == column // 16)).astype(BF16)
    for part in range(4):
        swapped = matmul(swap, bank[256 * part : 256 * part + 256, :]).astype(BF16)
        for c in range(CHANS):
            for h in range(4):
                natural[64 * h + 16 * part : 64 * h + 16 * part + 16, 128 * c : 128 * c + 128] = (
                    swapped[16 * c : 16 * c + 16, 128 * h : 128 * h + 128]
                )
    eye = (tile_iota(128, 128, 0) == tile_iota(128, 128, 1)).astype(BF16)
    for c in range(CHANS):
        turned = lax.dot_general(
            eye,
            natural[:, 128 * c : 128 * c + 128],
            (((1,), (1,)), ((), ())),
            preferred_element_type=F32,
        ).astype(BF16)
        for j in range(8):
            synthesis[16 * c : 16 * c + 16, 256 * j : 256 * j + 256] = turned[16 * j : 16 * j + 16, :]
    row, column = tile_iota(512, 512, 0), tile_iota(512, 512, 1)
    select = (
        (row // 128 == column // 32 % 4)
        & (row // 32 % 4 == column // 128)
        & (row % 32 == 31 - column % 32)
    ).astype(BF16)
    for cg in range(4):
        moved = matmul(natural[:, 512 * cg : 512 * cg + 512], select).astype(BF16)
        for h in range(4):
            for q in range(4):
                at = 128 * (4 * cg + h)
                gradient[64 * q : 64 * q + 64, at : at + 128] = moved[
                    64 * h : 64 * h + 64, 128 * q : 128 * q + 128
                ]


def shift_codes(codes, keep, shifted, place):
    width = codes.shape[1]
    for j in range(8):
        shifted[j, :, place : place + keep] = pltpu.roll(codes, width - (113 - 16 * j), 1)[:, :keep]


def synthesize(shifted, synthesis, spread, begin, end):
    for start in range(begin, end, 256):
        stop = min(start + 256, end)
        total = None
        for j in range(8):
            window = jnp.concatenate(
                [shifted[j, :, start - 128 * h + 384 : stop - 128 * h + 384] for h in range(4)], axis=0
            )
            part = matmul(synthesis[:, 256 * j : 256 * j + 256], window)
            total = part if total is None else total + part
        spread[:, start:stop] = total


def gather_rows(spread, begin):
    rows = []
    for c in range(CHANS):
        low = spread[16 * c : 16 * c + 8, begin : begin + 640]
        high = spread[16 * c + 8 : 16 * c + 16, begin : begin + 640]
        both = pltpu.roll(low, 640 - 15, 1, stride=1, stride_axis=0) + pltpu.roll(
            high, 640 - 7, 1, stride=1, stride_axis=0
        )
        rows.append(jnp.sum(both[:, :HALF], axis=0, keepdims=True))
    return jnp.concatenate(rows, axis=0)


def shift_misfit(misfit, first, last, drop, shifted):
    begin, end = 128 * (first + drop), 128 * last
    for c in range(CHANS):
        row = jnp.broadcast_to(misfit[c : c + 1, 128 * first : end], (16, end - 128 * first)).astype(BF16)
        near = pltpu.roll(row, 1, 1, stride=1, stride_axis=0)
        far = pltpu.roll(near, 16, 1)
        at = 32 * (c % 4)
        shifted[c // 4, at : at + 16, begin:end] = near[:, 128 * drop :]
        shifted[c // 4, at + 16 : at + 32, begin:end] = far[:, 128 * drop :]


def correlate(shifted, gradient, spread, begin, end):
    for start in range(begin, end, 256):
        stop = min(start + 256, end)
        total = None
        for cg in range(4):
            for h in (0, 2):
                window = jnp.concatenate(
                    [
                        shifted[cg, :, start + 128 * h : stop + 128 * h],
                        shifted[cg, :, start + 128 * h + 128 : stop + 128 * h + 128],
                    ],
                    axis=0,
                )
                at = 128 * (4 * cg + h)
                part = matmul(gradient[:, at : at + 256], window)
                total = part if total is None else total + part
        spread[:, start:stop] = total


def gather_taps(spread, begin):
    total = spread[192:256, begin + 128 : begin + 640]
    for q in range(3):
        rows = spread[64 * q : 64 * q + 64, begin : begin + 640]
        total = total + pltpu.roll(rows, 96 - 32 * q, 1)[:, 128:]
    return total


def column_of(row):
    diagonal = tile_iota(ATOMS, ATOMS, 0) == tile_iota(ATOMS, ATOMS, 1)
    return jnp.sum(jnp.where(diagonal, jnp.broadcast_to(row, (ATOMS, ATOMS)), 0.0), axis=1, keepdims=True)


def kernel(
    slabs,
    bank_hbm,
    codes_hbm,
    signal_hbm,
    step_size_hbm,
    threshold_hbm,
    out_codes,
    out_residual,
    bank,
    codes,
    signal,
    step_size,
    threshold,
    natural,
    synthesis,
    gradient,
    lowered,
    own,
    code_shift,
    spread,
    part,
    from_atom,
    from_next,
    misfit,
    misfit_shift,
    grad_send,
    grad_recv,
    code_send,
    scales,
    halo_sems,
    part_send,
    part_recv,
    grad_send_sem,
    grad_recv_sem,
    code_send_sem,
    code_recv_sem,
    edge_send_sem,
    edge_recv_sem,
    load_sems,
    word,
):
    tm, atom, me = lax.axis_index("tm"), lax.axis_index("atom"), lax.axis_index("chan")
    after, before = lax.rem(tm + 1, slabs), lax.rem(tm + slabs - 1, slabs)
    other = 1 - atom
    my_rows = pl.multiple_of(me // 4 * 16, 16)
    my_block = lax.rem(me, 4)

    barrier = pltpu.get_barrier_semaphore()

    def near(signal_one):
        for device in (
            {"tm": after},
            {"tm": before},
            {"atom": other},
            {"chan": me + 1 - 2 * lax.rem(me, 2)},
            {"chan": me + 2 - 4 * lax.rem(me // 2, 2)},
            {"chan": lax.rem(me + 4, GROUP)},
            {"chan": lax.rem(me + 8, GROUP)},
            {"chan": lax.rem(me + 12, GROUP)},
        ):
            signal_one(device)

    near(lambda device: pl.semaphore_signal(barrier, 1, device_id=device, device_id_type=MESH))
    loads = [
        pltpu.make_async_copy(source, target, load_sems.at[index])
        for index, (source, target) in enumerate(
            (
                (codes_hbm, codes),
                (bank_hbm, bank),
                (signal_hbm, signal),
                (step_size_hbm, step_size),
                (threshold_hbm, threshold),
            )
        )
    ]
    for load in loads:
        load.start()

    def spread_word(stage):
        near(
            lambda device: pl.semaphore_signal(
                word.at[stage], 1, device_id=device, device_id_type=MESH
            )
        )

    halo = pltpu.make_async_remote_copy(
        src_ref=lowered.at[2],
        dst_ref=lowered.at[0],
        send_sem=halo_sems.at[0],
        recv_sem=halo_sems.at[1],
        device_id={"tm": after},
        device_id_type=MESH,
    )

    loads[0].wait()
    for block in range(8):
        lowered[1 + block // 4, block % 4] = codes[:, 128 * block : 128 * block + 128].astype(BF16)
    for load in loads[1:]:
        load.wait()
    pl.semaphore_wait(barrier, 8)
    spread_word(0)
    halo.start()
    arrange_bank(bank, natural, synthesis, gradient)
    scales[:, 0:1] = column_of(step_size[...])
    scales[:, 1:2] = column_of(threshold[...])
    for half in range(2):
        at = pl.multiple_of((my_block + 4 * half) * 128, 128)
        own[half] = codes[pl.ds(my_rows, 16), pl.ds(at, 128)]

    def codes_of(first, last):
        return jnp.concatenate([lowered[b // 4, b % 4] for b in range(first, last)], axis=1)

    def late_half(sweep):
        shift_codes(codes_of(4, 12), 1024, code_shift, 512)
        synthesize(code_shift, synthesis, spread, 512, 1152)
        recon = gather_rows(spread, 512)
        part[sweep, 1] = recon - jnp.where(atom == 0, signal[:, HALF:].astype(F32), 0.0)

    def early_half(sweep):
        edge = jnp.where(tm > 0, codes_of(0, 4).astype(F32), 0.0).astype(BF16)
        shift_codes(jnp.concatenate([edge, lowered[1, 0]], axis=1), 512, code_shift, 0)
        synthesize(code_shift, synthesis, spread, 0, 512)
        recon = gather_rows(spread, 0)
        part[sweep, 0] = recon - jnp.where(atom == 0, signal[:, :HALF].astype(F32), 0.0)

    def part_copy(sweep, index, half, target, device):
        return pltpu.make_async_remote_copy(
            src_ref=part.at[sweep, half],
            dst_ref=target,
            send_sem=part_send.at[sweep, index],
            recv_sem=part_recv.at[sweep, index],
            device_id=device,
            device_id_type=MESH,
        )

    def grad_copy(half, turn):
        owner = lax.rem(me + turn, GROUP)
        return pltpu.make_async_remote_copy(
            src_ref=grad_send.at[half, owner],
            dst_ref=grad_recv.at[half, turn],
            send_sem=grad_send_sem.at[half, turn],
            recv_sem=grad_recv_sem.at[half, turn],
            device_id={"chan": owner},
            device_id_type=MESH,
        )

    def code_place(last, half):
        if last:
            at = pl.multiple_of((my_block + 4 * half) * 128, 128)
            return out_codes.at[pl.ds(my_rows, 16), pl.ds(at, 128)]
        return lowered.at[1 + half, my_block, pl.ds(my_rows, 16)]

    def code_copy(last, half, turn):
        return pltpu.make_async_remote_copy(
            src_ref=own.at[half] if last else code_send.at[half],
            dst_ref=code_place(last, half),
            send_sem=code_send_sem.at[half, turn],
            recv_sem=code_recv_sem.at[half, turn],
            device_id={"chan": lax.rem(me + turn, GROUP)},
            device_id_type=MESH,
        )

    def edge_copy(turn):
        return pltpu.make_async_remote_copy(
            src_ref=code_send.at[1],
            dst_ref=lowered.at[0, my_block, pl.ds(my_rows, 16)],
            send_sem=edge_send_sem.at[turn],
            recv_sem=edge_recv_sem.at[turn],
            device_id={"tm": after, "chan": lax.rem(me + turn, GROUP)},
            device_id_type=MESH,
        )

    def each(first, act):
        def run(turn, carry):
            act(turn)
            return carry

        lax.fori_loop(first, GROUP, run, 0)

    for sweep in range(ITERS):
        last = sweep == ITERS - 1
        copies = [
            part_copy(sweep, 0, 1, from_atom.at[sweep, 1], {"atom": other}),
            part_copy(sweep, 1, 0, from_atom.at[sweep, 0], {"atom": other}),
            part_copy(sweep, 2, 0, from_next.at[sweep, 0], {"tm": before}),
            part_copy(sweep, 3, 0, from_next.at[sweep, 1], {"tm": before, "atom": other}),
        ]
        late_half(sweep)
        copies[0].start()
        if sweep == 0:
            halo.wait()
            pl.semaphore_wait(word.at[0], 8)
            spread_word(1)
        else:
            each(0, lambda turn: edge_copy(turn).wait())
        early_half(sweep)
        for copy in (copies[3], copies[2], copies[1]):
            copy.start()

        copies[0].wait_recv()
        whole = part[sweep, 1] + from_atom[sweep, 1]
        misfit[:, HALF:SLAB] = whole
        if last:
            out_residual[:, HALF:SLAB] = whole
        shift_misfit(misfit, 4, 8, 1, misfit_shift)
        copies[1].wait_recv()
        whole = part[sweep, 0] + from_atom[sweep, 0]
        misfit[:, :HALF] = whole
        if last:
            out_residual[:, :HALF] = whole
        shift_misfit(misfit, 0, 5, 0, misfit_shift)
        correlate(misfit_shift, gradient, spread, 0, 640)

        def put(half):
            total = gather_taps(spread, HALF * half)
            for owner in range(GROUP):
                row, block = owner // 4 * 16, owner % 4 * 128
                grad_send[half, owner] = total[row : row + 16, block : block + 128]
            if sweep == 0 and half == 0:
                pl.semaphore_wait(word.at[1], 8)
                spread_word(2)
            each(1, lambda turn: grad_copy(half, turn).start())

        put(0)
        copies[2].wait_recv()
        copies[3].wait_recv()
        whole = from_next[sweep, 0] + from_next[sweep, 1]
        misfit[:, SLAB:] = jnp.where(tm < slabs - 1, whole, 0.0)
        shift_misfit(misfit, 7, 12, 1, misfit_shift)
        correlate(misfit_shift, gradient, spread, 640, 1152)
        put(1)

        for half in range(2):
            each(1, lambda turn: grad_copy(half, turn).wait_recv())
            total = grad_send[half, me]
            for turn in range(1, GROUP):
                total = total + grad_recv[half, turn]
            step = scales[pl.ds(my_rows, 16), 0:1]
            bound = step * scales[pl.ds(my_rows, 16), 1:2]
            moved = own[half] - step * total
            updated = moved - jnp.clip(moved, -bound, bound)
            own[half] = updated
            if not last:
                code_send[half] = updated.astype(BF16)
            each(1, lambda turn: code_copy(last, half, turn).start())
            if half == 1 and not last:
                pl.semaphore_wait(word.at[2], 8)
                each(0, lambda turn: edge_copy(turn).start())
            code_place(last, half)[...] = updated if last else updated.astype(BF16)
        for half in range(2):
            each(1, lambda turn: code_copy(last, half, turn).wait())
            each(1, lambda turn: grad_copy(half, turn).wait_send())
        for copy in copies:
            copy.wait_send()


def body(signal, codes_init, atom_bank, step_size, threshold):
    vmem = pl.BlockSpec(memory_space=pltpu.VMEM)
    return pl.pallas_call(
        functools.partial(kernel, lax.axis_size("tm")),
        out_shape=(
            jax.ShapeDtypeStruct((ATOMS, SLAB), F32),
            jax.ShapeDtypeStruct((CHANS, SLAB), F32),
        ),
        in_specs=[pl.BlockSpec(memory_space=pltpu.HBM)] * 5,
        out_specs=(vmem, vmem),
        scratch_shapes=[
            pltpu.VMEM((ATOMS * CHANS, TAPS), BF16),
            pltpu.VMEM((ATOMS, SLAB), F32),
            pltpu.VMEM((CHANS, SLAB), BF16),
            pltpu.VMEM((1, ATOMS), F32),
            pltpu.VMEM((1, ATOMS), F32),
            pltpu.VMEM((256, 2048), BF16),
            pltpu.VMEM((256, 2048), BF16),
            pltpu.VMEM((256, 2048), BF16),
            pltpu.VMEM((3, 4, ATOMS, LANES), BF16),
            pltpu.VMEM((2, 16, LANES), F32),
            pltpu.VMEM((8, ATOMS, 1536), BF16),
            pltpu.VMEM((256, 1152), F32),
            pltpu.VMEM((ITERS, 2, CHANS, HALF), F32),
            pltpu.VMEM((ITERS, 2, CHANS, HALF), F32),
            pltpu.VMEM((ITERS, 2, CHANS, HALF), F32),
            pltpu.VMEM((CHANS, 1536), F32),
            pltpu.VMEM((4, 128, 1536), BF16),
            pltpu.VMEM((2, GROUP, 16, LANES), F32),
            pltpu.VMEM((2, GROUP, 16, LANES), F32),
            pltpu.VMEM((2, 16, LANES), BF16),
            pltpu.VMEM((ATOMS, LANES), F32),
            pltpu.SemaphoreType.DMA((2,)),
            pltpu.SemaphoreType.DMA((ITERS, 4)),
            pltpu.SemaphoreType.DMA((ITERS, 4)),
            pltpu.SemaphoreType.DMA((2, GROUP)),
            pltpu.SemaphoreType.DMA((2, GROUP)),
            pltpu.SemaphoreType.DMA((2, GROUP)),
            pltpu.SemaphoreType.DMA((2, GROUP)),
            pltpu.SemaphoreType.DMA((GROUP,)),
            pltpu.SemaphoreType.DMA((GROUP,)),
            pltpu.SemaphoreType.DMA((5,)),
            pltpu.SemaphoreType.REGULAR((3,)),
        ],
        compiler_params=pltpu.CompilerParams(
            collective_id=0, has_side_effects=True, vmem_limit_bytes=48 * 1024 * 1024
        ),
    )(
        *(
            pltpu.with_memory_space_constraint(value, pltpu.HBM)
            for value in (
                atom_bank.reshape(ATOMS * CHANS, TAPS),
                codes_init,
                signal,
                step_size.reshape(1, ATOMS),
                threshold.reshape(1, ATOMS),
            )
        )
    )


def solution(mesh):
    placed = (P("chan", "tm"), P("atom", "tm"), P("atom", "chan", None), P("atom"), P("atom"))
    return jax.shard_map(
        body,
        mesh=mesh,
        in_specs=placed,
        out_specs=(P("atom", "tm"), P("chan", "tm")),
        check_vma=False,
    )
```

```python
import functools

import jax
import jax.numpy as jnp
from jax import lax
from jax.experimental import pallas as pl
from jax.experimental.pallas import tpu as pltpu
from jax.sharding import PartitionSpec as P

F32, BF16 = jnp.float32, jnp.bfloat16
MESH = pl.DeviceIdType.MESH
ITERS = 2
ATOMS, CHANS, TAPS, SLAB = 64, 16, 512, 1024
LANES, HALF = 128, 512
GRAD_SCALE, CODE_SCALE = 2.0**-8, 2.0**-12
GROUP = 16


def tile_iota(rows, columns, dimension):
    return lax.broadcasted_iota(jnp.int32, (rows, columns), dimension)


def matmul(left, right):
    return jnp.dot(left, right, preferred_element_type=F32)


def arrange_bank(bank, natural, synthesis, gradient):
    row, column = tile_iota(256, 256, 0), tile_iota(256, 256, 1)
    swap = ((row // 16 == column % 16) & (row % 16 == column // 16)).astype(BF16)
    for part in range(4):
        swapped = matmul(swap, bank[256 * part : 256 * part + 256, :]).astype(BF16)
        for c in range(CHANS):
            for h in range(4):
                natural[64 * h + 16 * part : 64 * h + 16 * part + 16, 128 * c : 128 * c + 128] = (
                    swapped[16 * c : 16 * c + 16, 128 * h : 128 * h + 128]
                )
    eye = (tile_iota(128, 128, 0) == tile_iota(128, 128, 1)).astype(BF16)
    for c in range(CHANS):
        turned = lax.dot_general(
            eye,
            natural[:, 128 * c : 128 * c + 128],
            (((1,), (1,)), ((), ())),
            preferred_element_type=F32,
        ).astype(BF16)
        for j in range(8):
            synthesis[16 * c : 16 * c + 16, 256 * j : 256 * j + 256] = turned[16 * j : 16 * j + 16, :]
    row, column = tile_iota(512, 512, 0), tile_iota(512, 512, 1)
    select = (
        (row // 128 == column // 32 % 4)
        & (row // 32 % 4 == column // 128)
        & (row % 32 == 31 - column % 32)
    ).astype(BF16)
    for cg in range(4):
        moved = matmul(natural[:, 512 * cg : 512 * cg + 512], select).astype(BF16)
        for h in range(4):
            for q in range(4):
                at = 128 * (4 * cg + h)
                gradient[64 * q : 64 * q + 64, at : at + 128] = moved[
                    64 * h : 64 * h + 64, 128 * q : 128 * q + 128
                ]


def shift_codes(codes, keep, shifted, place):
    width = codes.shape[1]
    for j in range(8):
        shifted[j, :, place : place + keep] = pltpu.roll(codes, width - (113 - 16 * j), 1)[:, :keep]


def synthesize(shifted, synthesis, spread, begin, end):
    for start in range(begin, end, 256):
        stop = min(start + 256, end)
        total = None
        for j in range(8):
            window = jnp.concatenate(
                [shifted[j, :, start - 128 * h + 384 : stop - 128 * h + 384] for h in range(4)], axis=0
            )
            part = matmul(synthesis[:, 256 * j : 256 * j + 256], window)
            total = part if total is None else total + part
        spread[:, start:stop] = total


def gather_rows(spread, begin):
    rows = []
    for c in range(CHANS):
        low = spread[16 * c : 16 * c + 8, begin : begin + 640]
        high = spread[16 * c + 8 : 16 * c + 16, begin : begin + 640]
        both = pltpu.roll(low, 640 - 15, 1, stride=1, stride_axis=0) + pltpu.roll(
            high, 640 - 7, 1, stride=1, stride_axis=0
        )
        rows.append(jnp.sum(both[:, :HALF], axis=0, keepdims=True))
    return jnp.concatenate(rows, axis=0)


def shift_misfit(misfit, first, last, drop, shifted):
    begin, end = 128 * (first + drop), 128 * last
    for c in range(CHANS):
        row = jnp.broadcast_to(misfit[c : c + 1, 128 * first : end], (16, end - 128 * first)).astype(BF16)
        near = pltpu.roll(row, 1, 1, stride=1, stride_axis=0)
        far = pltpu.roll(near, 16, 1)
        at = 32 * (c % 4)
        shifted[c // 4, at : at + 16, begin:end] = near[:, 128 * drop :]
        shifted[c // 4, at + 16 : at + 32, begin:end] = far[:, 128 * drop :]


def correlate(shifted, gradient, spread, begin, end):
    for start in range(begin, end, 256):
        stop = min(start + 256, end)
        total = None
        for cg in range(4):
            for h in (0, 2):
                window = jnp.concatenate(
                    [
                        shifted[cg, :, start + 128 * h : stop + 128 * h],
                        shifted[cg, :, start + 128 * h + 128 : stop + 128 * h + 128],
                    ],
                    axis=0,
                )
                at = 128 * (4 * cg + h)
                part = matmul(gradient[:, at : at + 256], window)
                total = part if total is None else total + part
        spread[:, start:stop] = total


def gather_taps(spread, begin):
    total = spread[192:256, begin + 128 : begin + 640]
    for q in range(3):
        rows = spread[64 * q : 64 * q + 64, begin : begin + 640]
        total = total + pltpu.roll(rows, 96 - 32 * q, 1)[:, 128:]
    return total


def encode(value, scale):
    scaled = value * scale
    return (scaled * scaled * scaled * jnp.abs(scaled)).astype(BF16)


def decode(code, scale):
    power = code.astype(F32)
    root = jnp.sqrt(jnp.sqrt(jnp.abs(power))) * (1.0 / scale)
    return jnp.where(power < 0.0, -root, root)


def column_of(row):
    diagonal = tile_iota(ATOMS, ATOMS, 0) == tile_iota(ATOMS, ATOMS, 1)
    return jnp.sum(jnp.where(diagonal, jnp.broadcast_to(row, (ATOMS, ATOMS)), 0.0), axis=1, keepdims=True)


def kernel(
    slabs,
    bank_hbm,
    codes_hbm,
    signal_hbm,
    step_size_hbm,
    threshold_hbm,
    out_codes,
    out_residual,
    bank,
    codes,
    signal,
    step_size,
    threshold,
    natural,
    synthesis,
    gradient,
    lowered,
    own,
    code_shift,
    spread,
    part,
    from_atom,
    from_next,
    misfit,
    misfit_shift,
    grad_send,
    grad_recv,
    code_send,
    scales,
    halo_sems,
    part_send,
    part_recv,
    grad_send_sem,
    grad_recv_sem,
    code_send_sem,
    code_recv_sem,
    edge_send_sem,
    edge_recv_sem,
    load_sems,
    word,
):
    tm, atom, me = lax.axis_index("tm"), lax.axis_index("atom"), lax.axis_index("chan")
    after, before = lax.rem(tm + 1, slabs), lax.rem(tm + slabs - 1, slabs)
    other = 1 - atom
    has_before, has_after = tm > 0, tm < slabs - 1
    near_count = 6 + has_before.astype(jnp.int32) + has_after.astype(jnp.int32)
    my_rows = pl.multiple_of(me // 4 * 16, 16)
    my_block = lax.rem(me, 4)

    barrier = pltpu.get_barrier_semaphore()

    def near(signal_one):
        @pl.when(has_after)
        def _():
            signal_one({"tm": after})

        @pl.when(has_before)
        def _():
            signal_one({"tm": before})

        for device in (
            {"atom": other},
            {"chan": me + 1 - 2 * lax.rem(me, 2)},
            {"chan": me + 2 - 4 * lax.rem(me // 2, 2)},
            {"chan": lax.rem(me + 4, GROUP)},
            {"chan": lax.rem(me + 8, GROUP)},
            {"chan": lax.rem(me + 12, GROUP)},
        ):
            signal_one(device)

    near(lambda device: pl.semaphore_signal(barrier, 1, device_id=device, device_id_type=MESH))
    loads = [
        pltpu.make_async_copy(source, target, load_sems.at[index])
        for index, (source, target) in enumerate(
            (
                (codes_hbm, codes),
                (bank_hbm, bank),
                (signal_hbm, signal),
                (step_size_hbm, step_size),
                (threshold_hbm, threshold),
            )
        )
    ]
    for load in loads:
        load.start()

    def spread_word(stage):
        near(
            lambda device: pl.semaphore_signal(
                word.at[stage], 1, device_id=device, device_id_type=MESH
            )
        )

    halo = pltpu.make_async_remote_copy(
        src_ref=lowered.at[2],
        dst_ref=lowered.at[0],
        send_sem=halo_sems.at[0],
        recv_sem=halo_sems.at[1],
        device_id={"tm": after},
        device_id_type=MESH,
    )

    @pl.when(jnp.logical_not(has_before))
    def _():
        lowered[0] = jnp.zeros_like(lowered[0])

    @pl.when(jnp.logical_not(has_after))
    def _():
        from_next[...] = jnp.zeros_like(from_next)

    loads[0].wait()
    for block in range(8):
        lowered[1 + block // 4, block % 4] = codes[:, 128 * block : 128 * block + 128].astype(BF16)
    for load in loads[1:]:
        load.wait()
    pl.semaphore_wait(barrier, near_count)
    spread_word(0)
    pl.when(has_after)(halo.start)
    arrange_bank(bank, natural, synthesis, gradient)
    scales[:, 0:1] = column_of(step_size[...])
    scales[:, 1:2] = column_of(threshold[...])
    for half in range(2):
        at = pl.multiple_of((my_block + 4 * half) * 128, 128)
        own[half] = codes[pl.ds(my_rows, 16), pl.ds(at, 128)]

    def codes_of(first, last):
        return jnp.concatenate([lowered[b // 4, b % 4] for b in range(first, last)], axis=1)

    def late_half(sweep):
        shift_codes(codes_of(4, 12), 1024, code_shift, 512)
        synthesize(code_shift, synthesis, spread, 512, 1152)
        recon = gather_rows(spread, 512)
        part[sweep, 1] = recon - jnp.where(atom == 0, signal[:, HALF:].astype(F32), 0.0)

    def early_half(sweep):
        shift_codes(codes_of(0, 5), 512, code_shift, 0)
        synthesize(code_shift, synthesis, spread, 0, 512)
        recon = gather_rows(spread, 0)
        part[sweep, 0] = recon - jnp.where(atom == 0, signal[:, :HALF].astype(F32), 0.0)

    def part_copy(sweep, index, half, target, device):
        return pltpu.make_async_remote_copy(
            src_ref=part.at[sweep, half],
            dst_ref=target,
            send_sem=part_send.at[sweep, index],
            recv_sem=part_recv.at[sweep, index],
            device_id=device,
            device_id_type=MESH,
        )

    def grad_copy(half, turn):
        owner = lax.rem(me + turn, GROUP)
        return pltpu.make_async_remote_copy(
            src_ref=grad_send.at[half, owner],
            dst_ref=grad_recv.at[half, turn],
            send_sem=grad_send_sem.at[half, turn],
            recv_sem=grad_recv_sem.at[half, turn],
            device_id={"chan": owner},
            device_id_type=MESH,
        )

    def code_place(last, half):
        if last:
            at = pl.multiple_of((my_block + 4 * half) * 128, 128)
            return out_codes.at[pl.ds(my_rows, 16), pl.ds(at, 128)]
        return lowered.at[1 + half, my_block, pl.ds(my_rows, 16)]

    def code_copy(last, half, turn):
        return pltpu.make_async_remote_copy(
            src_ref=code_send.at[half],
            dst_ref=code_place(last, half),
            send_sem=code_send_sem.at[half, turn],
            recv_sem=code_recv_sem.at[half, turn],
            device_id={"chan": lax.rem(me + turn, GROUP)},
            device_id_type=MESH,
        )

    def edge_copy(turn):
        return pltpu.make_async_remote_copy(
            src_ref=code_send.at[1],
            dst_ref=lowered.at[0, my_block, pl.ds(my_rows, 16)],
            send_sem=edge_send_sem.at[turn],
            recv_sem=edge_recv_sem.at[turn],
            device_id={"tm": after, "chan": lax.rem(me + turn, GROUP)},
            device_id_type=MESH,
        )

    def each(first, act):
        def run(turn, carry):
            act(turn)
            return carry

        lax.fori_loop(first, GROUP, run, 0)

    for sweep in range(ITERS):
        last = sweep == ITERS - 1
        copies = [
            part_copy(sweep, 0, 1, from_atom.at[sweep, 1], {"atom": other}),
            part_copy(sweep, 1, 0, from_atom.at[sweep, 0], {"atom": other}),
            part_copy(sweep, 2, 0, from_next.at[sweep, 0], {"tm": before}),
            part_copy(sweep, 3, 0, from_next.at[sweep, 1], {"tm": before, "atom": other}),
        ]
        late_half(sweep)
        copies[0].start()
        if sweep == 0:
            pl.when(has_before)(halo.wait_recv)
            pl.when(has_after)(halo.wait_send)
            pl.semaphore_wait(word.at[0], near_count)
            spread_word(1)
        else:
            pl.when(has_before)(lambda: each(0, lambda turn: edge_copy(turn).wait_recv()))
        early_half(sweep)
        pl.when(has_before)(copies[3].start)
        pl.when(has_before)(copies[2].start)
        copies[1].start()

        copies[0].wait_recv()
        whole = part[sweep, 1] + from_atom[sweep, 1]
        misfit[:, HALF:SLAB] = whole
        if last:
            out_residual[:, HALF:SLAB] = whole
        shift_misfit(misfit, 4, 8, 1, misfit_shift)
        copies[1].wait_recv()
        whole = part[sweep, 0] + from_atom[sweep, 0]
        misfit[:, :HALF] = whole
        if last:
            out_residual[:, :HALF] = whole
        shift_misfit(misfit, 0, 5, 0, misfit_shift)
        correlate(misfit_shift, gradient, spread, 0, 640)

        def put(half):
            total = gather_taps(spread, HALF * half)
            for owner in range(GROUP):
                row, block = owner // 4 * 16, owner % 4 * 128
                piece = total[row : row + 16, block : block + 128]
                grad_send[half, owner] = encode(piece, GRAD_SCALE)
            if sweep == 0 and half == 0:
                pl.semaphore_wait(word.at[1], near_count)
                spread_word(2)
            each(1, lambda turn: grad_copy(half, turn).start())

        put(0)
        pl.when(has_after)(copies[2].wait_recv)
        pl.when(has_after)(copies[3].wait_recv)
        misfit[:, SLAB:] = from_next[sweep, 0] + from_next[sweep, 1]
        shift_misfit(misfit, 7, 12, 1, misfit_shift)
        correlate(misfit_shift, gradient, spread, 640, 1152)
        put(1)

        for half in range(2):
            each(1, lambda turn: grad_copy(half, turn).wait_recv())
            total = decode(grad_send[half, me], GRAD_SCALE)
            for turn in range(1, GROUP):
                total = total + decode(grad_recv[half, turn], GRAD_SCALE)
            step = scales[pl.ds(my_rows, 16), 0:1]
            bound = step * scales[pl.ds(my_rows, 16), 1:2]
            moved = own[half] - step * total
            updated = moved - jnp.clip(moved, -bound, bound)
            own[half] = updated
            code_send[half] = encode(updated, CODE_SCALE) if last else updated.astype(BF16)
            each(1, lambda turn: code_copy(last, half, turn).start())
            if half == 1 and not last:
                pl.semaphore_wait(word.at[2], near_count)
                pl.when(has_after)(lambda: each(0, lambda turn: edge_copy(turn).start()))
            code_place(last, half)[...] = code_send[half]
        for half in range(2):
            each(1, lambda turn: code_copy(last, half, turn).wait())
            each(1, lambda turn: grad_copy(half, turn).wait_send())
        if not last:
            pl.when(has_after)(lambda: each(0, lambda turn: edge_copy(turn).wait_send()))
        copies[0].wait_send()
        copies[1].wait_send()
        pl.when(has_before)(copies[2].wait_send)
        pl.when(has_before)(copies[3].wait_send)


def body(signal, codes_init, atom_bank, step_size, threshold):
    vmem = pl.BlockSpec(memory_space=pltpu.VMEM)
    coded, residual = pl.pallas_call(
        functools.partial(kernel, lax.axis_size("tm")),
        out_shape=(
            jax.ShapeDtypeStruct((ATOMS, SLAB), BF16),
            jax.ShapeDtypeStruct((CHANS, SLAB), F32),
        ),
        in_specs=[pl.BlockSpec(memory_space=pltpu.HBM)] * 5,
        out_specs=(vmem, vmem),
        scratch_shapes=[
            pltpu.VMEM((ATOMS * CHANS, TAPS), BF16),
            pltpu.VMEM((ATOMS, SLAB), F32),
            pltpu.VMEM((CHANS, SLAB), BF16),
            pltpu.VMEM((1, ATOMS), F32),
            pltpu.VMEM((1, ATOMS), F32),
            pltpu.VMEM((256, 2048), BF16),
            pltpu.VMEM((256, 2048), BF16),
            pltpu.VMEM((256, 2048), BF16),
            pltpu.VMEM((3, 4, ATOMS, LANES), BF16),
            pltpu.VMEM((2, 16, LANES), F32),
            pltpu.VMEM((8, ATOMS, 1536), BF16),
            pltpu.VMEM((256, 1152), F32),
            pltpu.VMEM((ITERS, 2, CHANS, HALF), F32),
            pltpu.VMEM((ITERS, 2, CHANS, HALF), F32),
            pltpu.VMEM((ITERS, 2, CHANS, HALF), F32),
            pltpu.VMEM((CHANS, 1536), F32),
            pltpu.VMEM((4, 128, 1536), BF16),
            pltpu.VMEM((2, GROUP, 16, LANES), BF16),
            pltpu.VMEM((2, GROUP, 16, LANES), BF16),
            pltpu.VMEM((2, 16, LANES), BF16),
            pltpu.VMEM((ATOMS, LANES), F32),
            pltpu.SemaphoreType.DMA((2,)),
            pltpu.SemaphoreType.DMA((ITERS, 4)),
            pltpu.SemaphoreType.DMA((ITERS, 4)),
            pltpu.SemaphoreType.DMA((2, GROUP)),
            pltpu.SemaphoreType.DMA((2, GROUP)),
            pltpu.SemaphoreType.DMA((2, GROUP)),
            pltpu.SemaphoreType.DMA((2, GROUP)),
            pltpu.SemaphoreType.DMA((GROUP,)),
            pltpu.SemaphoreType.DMA((GROUP,)),
            pltpu.SemaphoreType.DMA((5,)),
            pltpu.SemaphoreType.REGULAR((3,)),
        ],
        compiler_params=pltpu.CompilerParams(
            collective_id=0, has_side_effects=True, vmem_limit_bytes=48 * 1024 * 1024
        ),
    )(
        *(
            pltpu.with_memory_space_constraint(value, pltpu.HBM)
            for value in (
                atom_bank.reshape(ATOMS * CHANS, TAPS),
                codes_init,
                signal,
                step_size.reshape(1, ATOMS),
                threshold.reshape(1, ATOMS),
            )
        )
    )
    return decode(coded, CODE_SCALE), residual


def solution(mesh):
    placed = (P("chan", "tm"), P("atom", "tm"), P("atom", "chan", None), P("atom"), P("atom"))
    return jax.shard_map(
        body,
        mesh=mesh,
        in_specs=placed,
        out_specs=(P("atom", "tm"), P("chan", "tm")),
        check_vma=False,
    )
```

```python
import functools

import jax
import jax.numpy as jnp
from jax import lax
from jax.experimental import pallas as pl
from jax.experimental.pallas import tpu as pltpu
from jax.sharding import PartitionSpec as P

F32, BF16 = jnp.float32, jnp.bfloat16
MESH = pl.DeviceIdType.MESH
ITERS = 2
ATOMS, CHANS, TAPS, SLAB = 64, 16, 512, 1024
LANES, HALF = 128, 512
GRAD_SCALE, CODE_SCALE = 2.0**-8, 2.0**-12
GROUP = 16
STEPS = [(y, x, core) for y, x in ((2, 1), (1, 1), (3, 1), (2, 0), (0, 1), (1, 0), (3, 0), (0, 0)) for core in (1, 0)]


def tile_iota(rows, columns, dimension):
    return lax.broadcasted_iota(jnp.int32, (rows, columns), dimension)


def matmul(left, right):
    return jnp.dot(left, right, preferred_element_type=F32)


def arrange_bank(bank, natural, synthesis, gradient):
    row, column = tile_iota(256, 256, 0), tile_iota(256, 256, 1)
    swap = ((row // 16 == column % 16) & (row % 16 == column // 16)).astype(BF16)
    for part in range(4):
        swapped = matmul(swap, bank[256 * part : 256 * part + 256, :]).astype(BF16)
        for c in range(CHANS):
            for h in range(4):
                natural[64 * h + 16 * part : 64 * h + 16 * part + 16, 128 * c : 128 * c + 128] = (
                    swapped[16 * c : 16 * c + 16, 128 * h : 128 * h + 128]
                )
    eye = (tile_iota(128, 128, 0) == tile_iota(128, 128, 1)).astype(BF16)
    for c in range(CHANS):
        turned = lax.dot_general(
            eye,
            natural[:, 128 * c : 128 * c + 128],
            (((1,), (1,)), ((), ())),
            preferred_element_type=F32,
        ).astype(BF16)
        for j in range(8):
            synthesis[16 * c : 16 * c + 16, 256 * j : 256 * j + 256] = turned[16 * j : 16 * j + 16, :]
    row, column = tile_iota(512, 512, 0), tile_iota(512, 512, 1)
    select = (
        (row // 128 == column // 32 % 4)
        & (row // 32 % 4 == column // 128)
        & (row % 32 == 31 - column % 32)
    ).astype(BF16)
    for cg in range(4):
        moved = matmul(natural[:, 512 * cg : 512 * cg + 512], select).astype(BF16)
        for h in range(4):
            for q in range(4):
                at = 128 * (4 * cg + h)
                gradient[64 * q : 64 * q + 64, at : at + 128] = moved[
                    64 * h : 64 * h + 64, 128 * q : 128 * q + 128
                ]


def shift_codes(codes, keep, shifted, place):
    width = codes.shape[1]
    for j in range(8):
        shifted[j, :, place : place + keep] = pltpu.roll(codes, width - (113 - 16 * j), 1)[:, :keep]


def synthesize(shifted, synthesis, spread, begin, end):
    for start in range(begin, end, 256):
        stop = min(start + 256, end)
        total = None
        for j in range(8):
            window = jnp.concatenate(
                [shifted[j, :, start - 128 * h + 384 : stop - 128 * h + 384] for h in range(4)], axis=0
            )
            part = matmul(synthesis[:, 256 * j : 256 * j + 256], window)
            total = part if total is None else total + part
        spread[:, start:stop] = total


def gather_rows(spread, begin):
    rows = []
    for c in range(CHANS):
        low = spread[16 * c : 16 * c + 8, begin : begin + 640]
        high = spread[16 * c + 8 : 16 * c + 16, begin : begin + 640]
        both = pltpu.roll(low, 640 - 15, 1, stride=1, stride_axis=0) + pltpu.roll(
            high, 640 - 7, 1, stride=1, stride_axis=0
        )
        rows.append(jnp.sum(both[:, :HALF], axis=0, keepdims=True))
    return jnp.concatenate(rows, axis=0)


def shift_misfit(misfit, first, last, drop, shifted):
    begin, end = 128 * (first + drop), 128 * last
    for c in range(CHANS):
        row = jnp.broadcast_to(misfit[c : c + 1, 128 * first : end], (16, end - 128 * first)).astype(BF16)
        near = pltpu.roll(row, 1, 1, stride=1, stride_axis=0)
        far = pltpu.roll(near, 16, 1)
        at = 32 * (c % 4)
        shifted[c // 4, at : at + 16, begin:end] = near[:, 128 * drop :]
        shifted[c // 4, at + 16 : at + 32, begin:end] = far[:, 128 * drop :]


def correlate(shifted, gradient, spread, begin, end):
    for start in range(begin, end, 256):
        stop = min(start + 256, end)
        total = None
        for cg in range(4):
            for h in (0, 2):
                window = jnp.concatenate(
                    [
                        shifted[cg, :, start + 128 * h : stop + 128 * h],
                        shifted[cg, :, start + 128 * h + 128 : stop + 128 * h + 128],
                    ],
                    axis=0,
                )
                at = 128 * (4 * cg + h)
                part = matmul(gradient[:, at : at + 256], window)
                total = part if total is None else total + part
        spread[:, start:stop] = total


def gather_taps(spread, begin):
    total = spread[192:256, begin + 128 : begin + 640]
    for q in range(3):
        rows = spread[64 * q : 64 * q + 64, begin : begin + 640]
        total = total + pltpu.roll(rows, 96 - 32 * q, 1)[:, 128:]
    return total


def encode(value, scale):
    scaled = value * scale
    return (scaled * scaled * scaled * jnp.abs(scaled)).astype(BF16)


def decode(code, scale):
    power = code.astype(F32)
    root = jnp.sqrt(jnp.sqrt(jnp.abs(power))) * (1.0 / scale)
    return jnp.where(power < 0.0, -root, root)


def column_of(row):
    diagonal = tile_iota(ATOMS, ATOMS, 0) == tile_iota(ATOMS, ATOMS, 1)
    return jnp.sum(jnp.where(diagonal, jnp.broadcast_to(row, (ATOMS, ATOMS)), 0.0), axis=1, keepdims=True)


def kernel(
    slabs,
    bank_hbm,
    codes_hbm,
    signal_hbm,
    step_size_hbm,
    threshold_hbm,
    out_codes,
    out_residual,
    bank,
    codes,
    signal,
    step_size,
    threshold,
    natural,
    synthesis,
    gradient,
    lowered,
    own,
    code_shift,
    spread,
    part,
    from_atom,
    from_next,
    misfit,
    misfit_shift,
    grad_send,
    grad_recv,
    code_send,
    scales,
    halo_sems,
    part_send,
    part_recv,
    grad_send_sem,
    grad_recv_sem,
    code_send_sem,
    code_recv_sem,
    edge_send_sem,
    edge_recv_sem,
    load_sems,
    word,
):
    tm, atom, me = lax.axis_index("tm"), lax.axis_index("atom"), lax.axis_index("chan")
    after, before = lax.rem(tm + 1, slabs), lax.rem(tm + slabs - 1, slabs)
    other = 1 - atom
    has_before, has_after = tm > 0, tm < slabs - 1
    near_count = 6 + has_before.astype(jnp.int32) + has_after.astype(jnp.int32)
    my_rows = pl.multiple_of(me // 4 * 16, 16)
    my_block = lax.rem(me, 4)

    def at_step(step):
        y, x, core = step
        return (
            lax.rem(me // 4 + y, 4) * 4 + lax.rem(me // 2 + x, 2) * 2 + lax.rem(me + core, 2)
        )

    def slot(step):
        return step[0] * 4 + step[1] * 2 + step[2]

    barrier = pltpu.get_barrier_semaphore()

    def near(signal_one):
        @pl.when(has_after)
        def _():
            signal_one({"tm": after})

        @pl.when(has_before)
        def _():
            signal_one({"tm": before})

        for device in (
            {"atom": other},
            {"chan": me + 1 - 2 * lax.rem(me, 2)},
            {"chan": me + 2 - 4 * lax.rem(me // 2, 2)},
            {"chan": lax.rem(me + 4, GROUP)},
            {"chan": lax.rem(me + 8, GROUP)},
            {"chan": lax.rem(me + 12, GROUP)},
        ):
            signal_one(device)

    near(lambda device: pl.semaphore_signal(barrier, 1, device_id=device, device_id_type=MESH))
    loads = [
        pltpu.make_async_copy(source, target, load_sems.at[index])
        for index, (source, target) in enumerate(
            (
                (codes_hbm, codes),
                (bank_hbm, bank),
                (signal_hbm, signal),
                (step_size_hbm, step_size),
                (threshold_hbm, threshold),
            )
        )
    ]
    for load in loads:
        load.start()

    def spread_word(stage):
        near(
            lambda device: pl.semaphore_signal(
                word.at[stage], 1, device_id=device, device_id_type=MESH
            )
        )

    halo = pltpu.make_async_remote_copy(
        src_ref=lowered.at[2],
        dst_ref=lowered.at[0],
        send_sem=halo_sems.at[0],
        recv_sem=halo_sems.at[1],
        device_id={"tm": after},
        device_id_type=MESH,
    )

    @pl.when(jnp.logical_not(has_before))
    def _():
        lowered[0] = jnp.zeros_like(lowered[0])

    @pl.when(jnp.logical_not(has_after))
    def _():
        from_next[...] = jnp.zeros_like(from_next)

    loads[0].wait()
    for block in range(8):
        lowered[1 + block // 4, block % 4] = codes[:, 128 * block : 128 * block + 128].astype(BF16)
    for load in loads[1:]:
        load.wait()
    pl.semaphore_wait(barrier, near_count)
    spread_word(0)
    pl.when(has_after)(halo.start)
    arrange_bank(bank, natural, synthesis, gradient)
    scales[:, 0:1] = column_of(step_size[...])
    scales[:, 1:2] = column_of(threshold[...])
    for half in range(2):
        at = pl.multiple_of((my_block + 4 * half) * 128, 128)
        own[half] = codes[pl.ds(my_rows, 16), pl.ds(at, 128)]

    def codes_of(first, last):
        return jnp.concatenate([lowered[b // 4, b % 4] for b in range(first, last)], axis=1)

    def late_half(sweep):
        shift_codes(codes_of(4, 12), 1024, code_shift, 512)
        synthesize(code_shift, synthesis, spread, 512, 1152)
        recon = gather_rows(spread, 512)
        part[sweep, 1] = recon - jnp.where(atom == 0, signal[:, HALF:].astype(F32), 0.0)

    def early_half(sweep):
        shift_codes(codes_of(0, 5), 512, code_shift, 0)
        synthesize(code_shift, synthesis, spread, 0, 512)
        recon = gather_rows(spread, 0)
        part[sweep, 0] = recon - jnp.where(atom == 0, signal[:, :HALF].astype(F32), 0.0)

    def part_copy(sweep, index, half, target, device):
        return pltpu.make_async_remote_copy(
            src_ref=part.at[sweep, half],
            dst_ref=target,
            send_sem=part_send.at[sweep, index],
            recv_sem=part_recv.at[sweep, index],
            device_id=device,
            device_id_type=MESH,
        )

    def grad_copy(half, step):
        owner = at_step(step)
        return pltpu.make_async_remote_copy(
            src_ref=grad_send.at[half, owner],
            dst_ref=grad_recv.at[half, slot(step)],
            send_sem=grad_send_sem.at[half],
            recv_sem=grad_recv_sem.at[half],
            device_id={"chan": owner},
            device_id_type=MESH,
        )

    def code_place(last, half):
        if last:
            at = pl.multiple_of((my_block + 4 * half) * 128, 128)
            return out_codes.at[pl.ds(my_rows, 16), pl.ds(at, 128)]
        return lowered.at[1 + half, my_block, pl.ds(my_rows, 16)]

    def code_copy(last, half, step):
        return pltpu.make_async_remote_copy(
            src_ref=code_send.at[half],
            dst_ref=code_place(last, half),
            send_sem=code_send_sem.at[half],
            recv_sem=code_recv_sem.at[half],
            device_id={"chan": at_step(step)},
            device_id_type=MESH,
        )

    def edge_copy(step):
        return pltpu.make_async_remote_copy(
            src_ref=code_send.at[1],
            dst_ref=lowered.at[0, my_block, pl.ds(my_rows, 16)],
            send_sem=edge_send_sem,
            recv_sem=edge_recv_sem,
            device_id={"tm": after, "chan": at_step(step)},
            device_id_type=MESH,
        )

    others = [step for step in STEPS if slot(step)]

    def wait_pieces(sem, first):
        pieces = grad_recv.at[0, first:]
        pltpu.make_async_copy(pieces, pieces, sem).wait()

    def send_edges():
        for step in STEPS:
            edge_copy(step).start()

    sent = []
    for sweep in range(ITERS):
        last = sweep == ITERS - 1
        copies = [
            part_copy(sweep, 0, 1, from_atom.at[sweep, 1], {"atom": other}),
            part_copy(sweep, 1, 0, from_atom.at[sweep, 0], {"atom": other}),
            part_copy(sweep, 2, 0, from_next.at[sweep, 0], {"tm": before}),
            part_copy(sweep, 3, 0, from_next.at[sweep, 1], {"tm": before, "atom": other}),
        ]
        late_half(sweep)
        copies[0].start()
        sent.extend(copies)
        if sweep == 0:
            pl.when(has_before)(halo.wait_recv)
            pl.when(has_after)(halo.wait_send)
            pl.semaphore_wait(word.at[0], near_count)
            spread_word(1)
        else:
            pl.when(has_before)(lambda: wait_pieces(edge_recv_sem, 0))
        early_half(sweep)
        pl.when(has_before)(copies[3].start)
        pl.when(has_before)(copies[2].start)
        copies[1].start()

        copies[0].wait_recv()
        whole = part[sweep, 1] + from_atom[sweep, 1]
        misfit[:, HALF:SLAB] = whole
        if last:
            out_residual[:, HALF:SLAB] = whole
        shift_misfit(misfit, 4, 8, 1, misfit_shift)
        copies[1].wait_recv()
        whole = part[sweep, 0] + from_atom[sweep, 0]
        misfit[:, :HALF] = whole
        if last:
            out_residual[:, :HALF] = whole
        shift_misfit(misfit, 0, 5, 0, misfit_shift)
        correlate(misfit_shift, gradient, spread, 0, 640)

        def put(half):
            total = gather_taps(spread, HALF * half)
            if last:
                wait_pieces(grad_send_sem.at[half], 1)
            for owner in range(GROUP):
                row, block = owner // 4 * 16, owner % 4 * 128
                piece = total[row : row + 16, block : block + 128]
                grad_send[half, owner] = encode(piece, GRAD_SCALE)
            if sweep == 0 and half == 0:
                pl.semaphore_wait(word.at[1], near_count)
                spread_word(2)
            for step in others:
                grad_copy(half, step).start()

        put(0)
        pl.when(has_after)(copies[2].wait_recv)
        pl.when(has_after)(copies[3].wait_recv)
        misfit[:, SLAB:] = from_next[sweep, 0] + from_next[sweep, 1]
        shift_misfit(misfit, 7, 12, 1, misfit_shift)
        correlate(misfit_shift, gradient, spread, 640, 1152)
        put(1)

        for half in range(2):
            wait_pieces(grad_recv_sem.at[half], 1)
            total = decode(grad_send[half, me], GRAD_SCALE)
            for turn in range(1, GROUP):
                total = total + decode(grad_recv[half, turn], GRAD_SCALE)
            step = scales[pl.ds(my_rows, 16), 0:1]
            bound = step * scales[pl.ds(my_rows, 16), 1:2]
            moved = own[half] - step * total
            updated = moved - jnp.clip(moved, -bound, bound)
            own[half] = updated
            if last:
                wait_pieces(code_send_sem.at[half], 1)
                if half == 1:
                    pl.when(has_after)(lambda: wait_pieces(edge_send_sem, 0))
            code_send[half] = encode(updated, CODE_SCALE) if last else updated.astype(BF16)
            for step in others:
                code_copy(last, half, step).start()
            if half == 1 and not last:
                pl.semaphore_wait(word.at[2], near_count)
                pl.when(has_after)(send_edges)
            code_place(last, half)[...] = code_send[half]
        for half in range(2):
            wait_pieces(code_recv_sem.at[half], 1)
        if last:
            for half in range(2):
                wait_pieces(code_send_sem.at[half], 1)
                wait_pieces(grad_send_sem.at[half], 1)
            for index, copy in enumerate(sent):
                if index % 4 < 2:
                    copy.wait_send()
                else:
                    pl.when(has_before)(copy.wait_send)


def write_out(coded, residual, out_codes, out_residual, plain, sems):
    copies = [pltpu.make_async_copy(residual, out_residual, sems.at[4])]
    copies[0].start()
    for part in range(4):
        rows = pl.ds(16 * part, 16)
        plain[rows, :] = decode(coded[rows, :], CODE_SCALE)
        copies.append(pltpu.make_async_copy(plain.at[rows], out_codes.at[rows], sems.at[part]))
        copies[-1].start()
    for copy in copies:
        copy.wait()


def body(signal, codes_init, atom_bank, step_size, threshold):
    vmem = pl.BlockSpec(memory_space=pltpu.VMEM)
    coded, residual = pl.pallas_call(
        functools.partial(kernel, lax.axis_size("tm")),
        out_shape=(
            jax.ShapeDtypeStruct((ATOMS, SLAB), BF16),
            jax.ShapeDtypeStruct((CHANS, SLAB), F32),
        ),
        in_specs=[pl.BlockSpec(memory_space=pltpu.HBM)] * 5,
        out_specs=(vmem, vmem),
        scratch_shapes=[
            pltpu.VMEM((ATOMS * CHANS, TAPS), BF16),
            pltpu.VMEM((ATOMS, SLAB), F32),
            pltpu.VMEM((CHANS, SLAB), BF16),
            pltpu.VMEM((1, ATOMS), F32),
            pltpu.VMEM((1, ATOMS), F32),
            pltpu.VMEM((256, 2048), BF16),
            pltpu.VMEM((256, 2048), BF16),
            pltpu.VMEM((256, 2048), BF16),
            pltpu.VMEM((3, 4, ATOMS, LANES), BF16),
            pltpu.VMEM((2, 16, LANES), F32),
            pltpu.VMEM((8, ATOMS, 1536), BF16),
            pltpu.VMEM((256, 1152), F32),
            pltpu.VMEM((ITERS, 2, CHANS, HALF), F32),
            pltpu.VMEM((ITERS, 2, CHANS, HALF), F32),
            pltpu.VMEM((ITERS, 2, CHANS, HALF), F32),
            pltpu.VMEM((CHANS, 1536), F32),
            pltpu.VMEM((4, 128, 1536), BF16),
            pltpu.VMEM((2, GROUP, 16, LANES), BF16),
            pltpu.VMEM((2, GROUP, 16, LANES), BF16),
            pltpu.VMEM((2, 16, LANES), BF16),
            pltpu.VMEM((ATOMS, LANES), F32),
            pltpu.SemaphoreType.DMA((2,)),
            pltpu.SemaphoreType.DMA((ITERS, 4)),
            pltpu.SemaphoreType.DMA((ITERS, 4)),
            pltpu.SemaphoreType.DMA((2,)),
            pltpu.SemaphoreType.DMA((2,)),
            pltpu.SemaphoreType.DMA((2,)),
            pltpu.SemaphoreType.DMA((2,)),
            pltpu.SemaphoreType.DMA,
            pltpu.SemaphoreType.DMA,
            pltpu.SemaphoreType.DMA((5,)),
            pltpu.SemaphoreType.REGULAR((3,)),
        ],
        compiler_params=pltpu.CompilerParams(
            collective_id=0, has_side_effects=True, vmem_limit_bytes=48 * 1024 * 1024
        ),
    )(
        *(
            pltpu.with_memory_space_constraint(value, pltpu.HBM)
            for value in (
                atom_bank.reshape(ATOMS * CHANS, TAPS),
                codes_init,
                signal,
                step_size.reshape(1, ATOMS),
                threshold.reshape(1, ATOMS),
            )
        )
    )
    return pl.pallas_call(
        write_out,
        out_shape=(
            jax.ShapeDtypeStruct((ATOMS, SLAB), F32),
            jax.ShapeDtypeStruct((CHANS, SLAB), F32),
        ),
        in_specs=[vmem] * 2,
        out_specs=[pl.BlockSpec(memory_space=pltpu.HBM)] * 2,
        scratch_shapes=[pltpu.VMEM((ATOMS, SLAB), F32), pltpu.SemaphoreType.DMA((5,))],
    )(
        pltpu.with_memory_space_constraint(coded, pltpu.VMEM),
        pltpu.with_memory_space_constraint(residual, pltpu.VMEM),
    )


def solution(mesh):
    placed = (P("chan", "tm"), P("atom", "tm"), P("atom", "chan", None), P("atom"), P("atom"))
    return jax.shard_map(
        body,
        mesh=mesh,
        in_specs=placed,
        out_specs=(P("atom", "tm"), P("chan", "tm")),
        check_vma=False,
    )
```

```python
import functools

import jax
import jax.numpy as jnp
from jax import lax
from jax.experimental import pallas as pl
from jax.experimental.pallas import tpu as pltpu
from jax.sharding import PartitionSpec as P

F32, BF16 = jnp.float32, jnp.bfloat16
MESH = pl.DeviceIdType.MESH
ITERS = 2
ATOMS, CHANS, TAPS, SLAB = 64, 16, 512, 1024
LANES, HALF = 128, 512
GRAD_SCALE, CODE_SCALE = 2.0**-8, 2.0**-12
GROUP = 16
STEPS = [(y, x, core) for y, x in ((2, 1), (1, 1), (3, 1), (2, 0), (0, 1), (1, 0), (3, 0), (0, 0)) for core in (1, 0)]


def tile_iota(rows, columns, dimension):
    return lax.broadcasted_iota(jnp.int32, (rows, columns), dimension)


def matmul(left, right):
    return jnp.dot(left, right, preferred_element_type=F32)


def arrange_bank(bank, natural, synthesis, gradient):
    row, column = tile_iota(256, 256, 0), tile_iota(256, 256, 1)
    swap = ((row // 16 == column % 16) & (row % 16 == column // 16)).astype(BF16)
    for part in range(4):
        swapped = matmul(swap, bank[256 * part : 256 * part + 256, :]).astype(BF16)
        for c in range(CHANS):
            for h in range(4):
                natural[64 * h + 16 * part : 64 * h + 16 * part + 16, 128 * c : 128 * c + 128] = (
                    swapped[16 * c : 16 * c + 16, 128 * h : 128 * h + 128]
                )
    eye = (tile_iota(128, 128, 0) == tile_iota(128, 128, 1)).astype(BF16)
    for c in range(CHANS):
        turned = lax.dot_general(
            eye,
            natural[:, 128 * c : 128 * c + 128],
            (((1,), (1,)), ((), ())),
            preferred_element_type=F32,
        ).astype(BF16)
        for j in range(8):
            for pair in range(2):
                at = 1024 * pair + 128 * j
                synthesis[16 * c : 16 * c + 16, at : at + 128] = turned[
                    16 * j : 16 * j + 16, 128 * pair : 128 * pair + 128
                ]
    row, column = tile_iota(512, 512, 0), tile_iota(512, 512, 1)
    select = (
        (row // 128 == column // 32 % 4)
        & (row // 32 % 4 == column // 128)
        & (row % 32 == 31 - column % 32)
    ).astype(BF16)
    for cg in range(4):
        moved = matmul(natural[:, 512 * cg : 512 * cg + 512], select).astype(BF16)
        for h in range(4):
            for q in range(4):
                at = 1024 * (h // 2) + 128 * (2 * cg + h % 2)
                gradient[64 * q : 64 * q + 64, at : at + 128] = moved[
                    64 * h : 64 * h + 64, 128 * q : 128 * q + 128
                ]


def shift_codes(codes, keep, shifted, place):
    width = codes.shape[1]
    for j in range(8):
        shifted[j, :, place : place + keep] = pltpu.roll(codes, width - (113 - 16 * j), 1)[:, :keep]


def multiply(weights, window_of, spread, begin, end, pairs, add):
    window = jnp.concatenate([piece for pair in pairs for piece in window_of(pair)], axis=0)
    total = matmul(weights[:, 1024 * pairs[0] : 1024 * pairs[-1] + 1024], window)
    spread[:, begin:end] = spread[:, begin:end] + total if add else total


def synthesize(shifted, synthesis, spread, begin, end, pairs=(0, 1), add=False):
    def window_of(pair):
        return [
            shifted[j, :, begin - 128 * h + 384 : end - 128 * h + 384]
            for j in range(8)
            for h in (2 * pair, 2 * pair + 1)
        ]

    multiply(synthesis, window_of, spread, begin, end, pairs, add)


def gather_rows(spread, begin):
    rows = []
    for c in range(CHANS):
        low = spread[16 * c : 16 * c + 8, begin : begin + 640]
        high = spread[16 * c + 8 : 16 * c + 16, begin : begin + 640]
        both = pltpu.roll(low, 640 - 15, 1, stride=1, stride_axis=0) + pltpu.roll(
            high, 640 - 7, 1, stride=1, stride_axis=0
        )
        rows.append(jnp.sum(both[:, :HALF], axis=0, keepdims=True))
    return jnp.concatenate(rows, axis=0)


def shift_misfit(misfit, first, last, drop, shifted):
    begin, end = 128 * (first + drop), 128 * last
    for c in range(CHANS):
        row = jnp.broadcast_to(misfit[c : c + 1, 128 * first : end], (16, end - 128 * first)).astype(BF16)
        near = pltpu.roll(row, 1, 1, stride=1, stride_axis=0)
        far = pltpu.roll(near, 16, 1)
        at = 32 * (c % 4)
        shifted[c // 4, at : at + 16, begin:end] = near[:, 128 * drop :]
        shifted[c // 4, at + 16 : at + 32, begin:end] = far[:, 128 * drop :]


def correlate(shifted, gradient, spread, begin, end, pairs=(0, 1), add=False):
    def window_of(pair):
        return [
            shifted[cg, :, begin + 128 * h : end + 128 * h]
            for cg in range(4)
            for h in (2 * pair, 2 * pair + 1)
        ]

    multiply(gradient, window_of, spread, begin, end, pairs, add)


def gather_taps(spread, begin):
    total = spread[192:256, begin + 128 : begin + 640]
    for q in range(3):
        rows = spread[64 * q : 64 * q + 64, begin : begin + 640]
        total = total + pltpu.roll(rows, 96 - 32 * q, 1)[:, 128:]
    return total


def encode(value, scale):
    scaled = value * scale
    return (scaled * scaled * scaled * jnp.abs(scaled)).astype(BF16)


def decode(code, scale):
    power = code.astype(F32)
    root = jnp.sqrt(jnp.sqrt(jnp.abs(power))) * (1.0 / scale)
    return jnp.where(power < 0.0, -root, root)


def column_of(row):
    diagonal = tile_iota(ATOMS, ATOMS, 0) == tile_iota(ATOMS, ATOMS, 1)
    return jnp.sum(jnp.where(diagonal, jnp.broadcast_to(row, (ATOMS, ATOMS)), 0.0), axis=1, keepdims=True)


def kernel(
    slabs,
    bank_hbm,
    codes_hbm,
    signal_hbm,
    step_size_hbm,
    threshold_hbm,
    out_codes,
    out_residual,
    bank,
    codes,
    signal_in,
    step_size,
    threshold,
    natural,
    synthesis,
    gradient,
    lowered,
    own,
    code_shift,
    spread,
    part,
    coded_part,
    from_atom,
    atom_tail,
    from_next,
    from_before,
    misfit,
    misfit_shift,
    grad_send,
    grad_recv,
    code_send,
    scales,
    part_send,
    part_recv,
    grad_send_sem,
    grad_recv_sem,
    code_send_sem,
    code_recv_sem,
    load_sems,
    word,
):
    tm, atom, me = lax.axis_index("tm"), lax.axis_index("atom"), lax.axis_index("chan")
    after, before = lax.rem(tm + 1, slabs), lax.rem(tm + slabs - 1, slabs)
    other = 1 - atom
    has_before, has_after = tm > 0, tm < slabs - 1
    ends = has_before.astype(jnp.int32) + has_after.astype(jnp.int32)
    my_rows = pl.multiple_of(me // 4 * 16, 16)
    my_block = lax.rem(me, 4)

    def at_step(step):
        y, x, core = step
        return (
            lax.rem(me // 4 + y, 4) * 4 + lax.rem(me // 2 + x, 2) * 2 + lax.rem(me + core, 2)
        )

    def slot(step):
        return step[0] * 4 + step[1] * 2 + step[2]

    barrier = pltpu.get_barrier_semaphore()

    def signal(semaphore, device):
        pl.semaphore_signal(semaphore, 1, device_id=device, device_id_type=MESH)

    def signal_group(semaphore):
        for step in ((0, 0, 1), (0, 1, 0), (1, 0, 0), (2, 0, 0), (3, 0, 0)):
            signal(semaphore, {"chan": at_step(step)})

    for present, slab in ((has_after, after), (has_before, before)):

        @pl.when(present)
        def _(slab=slab):
            signal(barrier, {"tm": slab, "atom": other})
            signal(barrier, {"tm": slab})

    signal_group(barrier)
    signal(barrier, {"atom": other})
    loads = [
        pltpu.make_async_copy(source, target, load_sems.at[index])
        for index, (source, target) in enumerate(
            (
                (codes_hbm, codes),
                (bank_hbm, bank),
                (signal_hbm, signal_in),
                (step_size_hbm, step_size),
                (threshold_hbm, threshold),
            )
        )
    ]
    for load in loads:
        load.start()

    @pl.when(jnp.logical_not(has_before))
    def _():
        from_before[...] = jnp.zeros_like(from_before)

    @pl.when(jnp.logical_not(has_after))
    def _():
        from_next[...] = jnp.zeros_like(from_next)

    loads[0].wait()
    for block in range(8):
        lowered[block // 4, block % 4] = codes[:, 128 * block : 128 * block + 128].astype(BF16)
    for load in loads[1:]:
        load.wait()
    arrange_bank(bank, natural, synthesis, gradient)
    scales[:, 0:1] = column_of(step_size[...])
    scales[:, 1:2] = column_of(threshold[...])
    for half in range(2):
        at = pl.multiple_of((my_block + 4 * half) * 128, 128)
        own[half] = codes[pl.ds(my_rows, 16), pl.ds(at, 128)]

    code_shift[:, :, 256:384] = jnp.zeros((8, ATOMS, LANES), BF16)
    code_shift[:, :, 1536:] = jnp.zeros((8, ATOMS, LANES), BF16)
    spread[:, 1536:] = jnp.zeros((256, LANES), F32)
    pl.semaphore_wait(barrier, 6 + 2 * ends)
    signal_group(word.at[0])

    nothing = jnp.zeros((ATOMS, LANES), BF16)

    def codes_of(first, last):
        return [lowered[b // 4, b % 4] for b in range(first, last)]

    def keep_part(sweep, which, recon):
        if which < 2:
            own_signal = signal_in[:, HALF * which : HALF * which + HALF].astype(F32)
            recon = recon - jnp.where(atom == 0, own_signal, 0.0)
        if which < 2:
            part[sweep, which] = recon
        if which != 1:
            coded_part[sweep, which // 2] = encode(recon, GRAD_SCALE)

    def early_half(sweep):
        shift_codes(jnp.concatenate([nothing, *codes_of(0, 4), nothing], axis=1), 640, code_shift, 384)
        synthesize(code_shift, synthesis, spread, 0, 256, (0,))
        synthesize(code_shift, synthesis, spread, 256, 512)
        synthesize(code_shift, synthesis, spread, 512, 640)
        keep_part(sweep, 0, gather_rows(spread, 0))

    def tail(sweep):
        shift_codes(jnp.concatenate([*codes_of(3, 8), nothing], axis=1), 640, code_shift, 896)
        synthesize(code_shift, synthesis, spread, 1024, 1280)
        synthesize(code_shift, synthesis, spread, 1280, 1536, (1,))
        keep_part(sweep, 2, gather_rows(spread, 1024))

    def late_half(sweep):
        synthesize(code_shift, synthesis, spread, 512, 768)
        synthesize(code_shift, synthesis, spread, 768, 1024)
        keep_part(sweep, 1, gather_rows(spread, 512))

    def part_copy(sweep, index, source, target, device):
        return pltpu.make_async_remote_copy(
            src_ref=source,
            dst_ref=target,
            send_sem=part_send.at[sweep, index],
            recv_sem=part_recv.at[sweep, index],
            device_id=device,
            device_id_type=MESH,
        )

    def grad_copy(half, step):
        owner = at_step(step)
        return pltpu.make_async_remote_copy(
            src_ref=grad_send.at[half, owner],
            dst_ref=grad_recv.at[half, slot(step)],
            send_sem=grad_send_sem.at[half],
            recv_sem=grad_recv_sem.at[half],
            device_id={"chan": owner},
            device_id_type=MESH,
        )

    def code_place(last, half):
        if last:
            at = pl.multiple_of((my_block + 4 * half) * 128, 128)
            return out_codes.at[pl.ds(my_rows, 16), pl.ds(at, 128)]
        return lowered.at[half, my_block, pl.ds(my_rows, 16)]

    def code_copy(last, half, step):
        return pltpu.make_async_remote_copy(
            src_ref=code_send.at[half],
            dst_ref=code_place(last, half),
            send_sem=code_send_sem.at[half],
            recv_sem=code_recv_sem.at[half],
            device_id={"chan": at_step(step)},
            device_id_type=MESH,
        )

    others = [step for step in STEPS if slot(step)]

    def wait_pieces(sem, first):
        pieces = grad_recv.at[0, first:]
        pltpu.make_async_copy(pieces, pieces, sem).wait()

    sent = []
    for sweep in range(ITERS):
        last = sweep == ITERS - 1
        copies = [
            part_copy(sweep, index, source, target, device)
            for index, (source, target, device) in enumerate(
                (
                    (coded_part.at[sweep, 0], from_next.at[sweep, 1], {"tm": before, "atom": other}),
                    (coded_part.at[sweep, 0], from_next.at[sweep, 0], {"tm": before}),
                    (part.at[sweep, 0], from_atom.at[sweep, 0], {"atom": other}),
                    (coded_part.at[sweep, 1], from_before.at[sweep, 1], {"tm": after, "atom": other}),
                    (coded_part.at[sweep, 1], from_before.at[sweep, 0], {"tm": after}),
                    (coded_part.at[sweep, 1], atom_tail.at[sweep], {"atom": other}),
                    (part.at[sweep, 1], from_atom.at[sweep, 1], {"atom": other}),
                )
            )
        ]

        def start(first, end):
            for index in range(first, end):
                if index < 2:
                    pl.when(has_before)(copies[index].start)
                elif index in (3, 4):
                    pl.when(has_after)(copies[index].start)
                else:
                    copies[index].start()

        if sweep:
            wait_pieces(code_recv_sem.at[0], 1)
        early_half(sweep)
        start(0, 3)
        if sweep:
            wait_pieces(code_recv_sem.at[1], 1)
        tail(sweep)
        start(3, 6)
        late_half(sweep)
        start(6, 7)
        sent.append(copies)
        if sweep == 0:
            pl.semaphore_wait(word.at[0], 5)
            signal_group(word.at[1])

        def both(one, two):
            return decode(one[...], GRAD_SCALE) + decode(two[...], GRAD_SCALE)

        pl.when(has_after)(copies[0].wait_recv)
        pl.when(has_after)(copies[1].wait_recv)
        copies[5].wait_recv()
        edge = both(from_next.at[sweep, 0], from_next.at[sweep, 1]) + both(
            coded_part.at[sweep, 1], atom_tail.at[sweep]
        )
        misfit[:, SLAB:] = jnp.where(has_after, edge, 0.0)
        copies[2].wait_recv()
        pl.when(has_before)(copies[3].wait_recv)
        pl.when(has_before)(copies[4].wait_recv)
        whole = (part[sweep, 0] + from_atom[sweep, 0]) + both(
            from_before.at[sweep, 0], from_before.at[sweep, 1]
        )
        misfit[:, :HALF] = whole
        if last:
            out_residual[:, :HALF] = whole
        copies[6].wait_recv()
        whole = part[sweep, 1] + from_atom[sweep, 1]
        misfit[:, HALF:SLAB] = whole
        if last:
            out_residual[:, HALF:SLAB] = whole
        shift_misfit(misfit, 0, 8, 0, misfit_shift)
        correlate(misfit_shift, gradient, spread, 0, 128)
        correlate(misfit_shift, gradient, spread, 128, 384)
        correlate(misfit_shift, gradient, spread, 384, 640)

        def put(half):
            total = gather_taps(spread, HALF * half)
            if last:
                wait_pieces(grad_send_sem.at[half], 1)
            for owner in range(GROUP):
                row, block = owner // 4 * 16, owner % 4 * 128
                piece = total[row : row + 16, block : block + 128]
                grad_send[half, owner] = encode(piece, GRAD_SCALE)
            if sweep == 0 and half == 0:
                pl.semaphore_wait(word.at[1], 5)
            for step in others:
                grad_copy(half, step).start()

        put(0)
        shift_misfit(misfit, 7, 12, 1, misfit_shift)
        correlate(misfit_shift, gradient, spread, 640, 896)
        correlate(misfit_shift, gradient, spread, 896, 1152)
        put(1)

        for half in range(2):
            wait_pieces(grad_recv_sem.at[half], 1)
            total = decode(grad_send[half, me], GRAD_SCALE)
            for turn in range(1, GROUP):
                total = total + decode(grad_recv[half, turn], GRAD_SCALE)
            step = scales[pl.ds(my_rows, 16), 0:1]
            bound = step * scales[pl.ds(my_rows, 16), 1:2]
            moved = own[half] - step * total
            updated = moved - jnp.clip(moved, -bound, bound)
            own[half] = updated
            if last:
                wait_pieces(code_send_sem.at[half], 1)
            code_send[half] = encode(updated, CODE_SCALE) if last else updated.astype(BF16)
            for step in others:
                code_copy(last, half, step).start()
            code_place(last, half)[...] = code_send[half]
        if last:
            for half in range(2):
                wait_pieces(code_recv_sem.at[half], 1)
                wait_pieces(code_send_sem.at[half], 1)
                wait_pieces(grad_send_sem.at[half], 1)
            for copy in (copy for group in sent for copy in group[:2]):
                pl.when(has_before)(copy.wait_send)
            for copy in (copy for group in sent for copy in group[3:5]):
                pl.when(has_after)(copy.wait_send)
            for group in sent:
                for index in (2, 5, 6):
                    group[index].wait_send()


def write_out(coded, residual, out_codes, out_residual, plain, sems):
    copies = [pltpu.make_async_copy(residual, out_residual, sems.at[4])]
    copies[0].start()
    for part in range(4):
        rows = pl.ds(16 * part, 16)
        plain[rows, :] = decode(coded[rows, :], CODE_SCALE)
        copies.append(pltpu.make_async_copy(plain.at[rows], out_codes.at[rows], sems.at[part]))
        copies[-1].start()
    for copy in copies:
        copy.wait()


def body(signal, codes_init, atom_bank, step_size, threshold):
    vmem = pl.BlockSpec(memory_space=pltpu.VMEM)
    coded, residual = pl.pallas_call(
        functools.partial(kernel, lax.axis_size("tm")),
        out_shape=(
            jax.ShapeDtypeStruct((ATOMS, SLAB), BF16),
            jax.ShapeDtypeStruct((CHANS, SLAB), F32),
        ),
        in_specs=[pl.BlockSpec(memory_space=pltpu.HBM)] * 5,
        out_specs=(vmem, vmem),
        scratch_shapes=[
            pltpu.VMEM((ATOMS * CHANS, TAPS), BF16),
            pltpu.VMEM((ATOMS, SLAB), F32),
            pltpu.VMEM((CHANS, SLAB), BF16),
            pltpu.VMEM((1, ATOMS), F32),
            pltpu.VMEM((1, ATOMS), F32),
            pltpu.VMEM((256, 2048), BF16),
            pltpu.VMEM((256, 2048), BF16),
            pltpu.VMEM((256, 2048), BF16),
            pltpu.VMEM((2, 4, ATOMS, LANES), BF16),
            pltpu.VMEM((2, 16, LANES), F32),
            pltpu.VMEM((8, ATOMS, 1664), BF16),
            pltpu.VMEM((256, 1664), F32),
            pltpu.VMEM((ITERS, 2, CHANS, HALF), F32),
            pltpu.VMEM((ITERS, 2, CHANS, HALF), BF16),
            pltpu.VMEM((ITERS, 2, CHANS, HALF), F32),
            pltpu.VMEM((ITERS, CHANS, HALF), BF16),
            pltpu.VMEM((ITERS, 2, CHANS, HALF), BF16),
            pltpu.VMEM((ITERS, 2, CHANS, HALF), BF16),
            pltpu.VMEM((CHANS, 1536), F32),
            pltpu.VMEM((4, 128, 1536), BF16),
            pltpu.VMEM((2, GROUP, 16, LANES), BF16),
            pltpu.VMEM((2, GROUP, 16, LANES), BF16),
            pltpu.VMEM((2, 16, LANES), BF16),
            pltpu.VMEM((ATOMS, LANES), F32),
            pltpu.SemaphoreType.DMA((ITERS, 7)),
            pltpu.SemaphoreType.DMA((ITERS, 7)),
            pltpu.SemaphoreType.DMA((2,)),
            pltpu.SemaphoreType.DMA((2,)),
            pltpu.SemaphoreType.DMA((2,)),
            pltpu.SemaphoreType.DMA((2,)),
            pltpu.SemaphoreType.DMA((5,)),
            pltpu.SemaphoreType.REGULAR((2,)),
        ],
        compiler_params=pltpu.CompilerParams(
            collective_id=0, has_side_effects=True, vmem_limit_bytes=48 * 1024 * 1024
        ),
    )(
        *(
            pltpu.with_memory_space_constraint(value, pltpu.HBM)
            for value in (
                atom_bank.reshape(ATOMS * CHANS, TAPS),
                codes_init,
                signal,
                step_size.reshape(1, ATOMS),
                threshold.reshape(1, ATOMS),
            )
        )
    )
    return pl.pallas_call(
        write_out,
        out_shape=(
            jax.ShapeDtypeStruct((ATOMS, SLAB), F32),
            jax.ShapeDtypeStruct((CHANS, SLAB), F32),
        ),
        in_specs=[vmem] * 2,
        out_specs=[pl.BlockSpec(memory_space=pltpu.HBM)] * 2,
        scratch_shapes=[pltpu.VMEM((ATOMS, SLAB), F32), pltpu.SemaphoreType.DMA((5,))],
    )(
        pltpu.with_memory_space_constraint(coded, pltpu.VMEM),
        pltpu.with_memory_space_constraint(residual, pltpu.VMEM),
    )


def solution(mesh):
    placed = (P("chan", "tm"), P("atom", "tm"), P("atom", "chan", None), P("atom"), P("atom"))
    return jax.shard_map(
        body,
        mesh=mesh,
        in_specs=placed,
        out_specs=(P("atom", "tm"), P("chan", "tm")),
        check_vma=False,
    )
```

```python
import functools

import jax
import jax.numpy as jnp
from jax import lax
from jax.experimental import pallas as pl
from jax.experimental.pallas import tpu as pltpu
from jax.sharding import PartitionSpec as P

F32, BF16 = jnp.float32, jnp.bfloat16
MESH = pl.DeviceIdType.MESH
ITERS = 2
ATOMS, CHANS, TAPS, SLAB = 64, 16, 512, 1024
LANES, HALF = 128, 512
GRAD_SCALE, CODE_SCALE = 2.0**-8, 2.0**-12
GROUP = 16
STEPS = [(y, x, core) for y, x in ((2, 1), (1, 1), (3, 1), (2, 0), (0, 1), (1, 0), (3, 0), (0, 0)) for core in (1, 0)]


def tile_iota(rows, columns, dimension):
    return lax.broadcasted_iota(jnp.int32, (rows, columns), dimension)


def matmul(left, right):
    return jnp.dot(left, right, preferred_element_type=F32)


def arrange_bank(bank, natural, synthesis, gradient):
    row, column = tile_iota(256, 256, 0), tile_iota(256, 256, 1)
    swap = ((row // 16 == column % 16) & (row % 16 == column // 16)).astype(BF16)
    for part in range(4):
        swapped = matmul(swap, bank[256 * part : 256 * part + 256, :]).astype(BF16)
        for c in range(CHANS):
            for h in range(4):
                natural[64 * h + 16 * part : 64 * h + 16 * part + 16, 128 * c : 128 * c + 128] = (
                    swapped[16 * c : 16 * c + 16, 128 * h : 128 * h + 128]
                )
    eye = (tile_iota(128, 128, 0) == tile_iota(128, 128, 1)).astype(BF16)
    for c in range(CHANS):
        turned = lax.dot_general(
            eye,
            natural[:, 128 * c : 128 * c + 128],
            (((1,), (1,)), ((), ())),
            preferred_element_type=F32,
        ).astype(BF16)
        for j in range(8):
            for pair in range(2):
                at = 1024 * pair + 128 * j
                synthesis[16 * c : 16 * c + 16, at : at + 128] = turned[
                    16 * j : 16 * j + 16, 128 * pair : 128 * pair + 128
                ]
    row, column = tile_iota(512, 512, 0), tile_iota(512, 512, 1)
    select = (
        (row // 128 == column // 32 % 4)
        & (row // 32 % 4 == column // 128)
        & (row % 32 == 31 - column % 32)
    ).astype(BF16)
    for cg in range(4):
        moved = matmul(natural[:, 512 * cg : 512 * cg + 512], select).astype(BF16)
        for h in range(4):
            for q in range(4):
                at = 1024 * (h // 2) + 128 * (2 * cg + h % 2)
                gradient[64 * q : 64 * q + 64, at : at + 128] = moved[
                    64 * h : 64 * h + 64, 128 * q : 128 * q + 128
                ]


def shift_codes(codes, keep, shifted, place):
    width = codes.shape[1]
    for j in range(8):
        shifted[j, :, place : place + keep] = pltpu.roll(codes, width - (113 - 16 * j), 1)[:, :keep]


def multiply(weights, window_of, spread, begin, end, pairs, add):
    window = jnp.concatenate([piece for pair in pairs for piece in window_of(pair)], axis=0)
    total = matmul(weights[:, 1024 * pairs[0] : 1024 * pairs[-1] + 1024], window)
    spread[:, begin:end] = spread[:, begin:end] + total if add else total


def synthesize(shifted, synthesis, spread, begin, end, pairs=(0, 1), add=False):
    def window_of(pair):
        return [
            shifted[j, :, begin - 128 * h + 384 : end - 128 * h + 384]
            for j in range(8)
            for h in (2 * pair, 2 * pair + 1)
        ]

    multiply(synthesis, window_of, spread, begin, end, pairs, add)


def gather_rows(spread, begin):
    rows = []
    for c in range(CHANS):
        low = spread[16 * c : 16 * c + 8, begin : begin + 640]
        high = spread[16 * c + 8 : 16 * c + 16, begin : begin + 640]
        both = pltpu.roll(low, 640 - 15, 1, stride=1, stride_axis=0) + pltpu.roll(
            high, 640 - 7, 1, stride=1, stride_axis=0
        )
        rows.append(jnp.sum(both[:, :HALF], axis=0, keepdims=True))
    return jnp.concatenate(rows, axis=0)


def shift_misfit(misfit, first, last, drop, shifted):
    begin, end = 128 * (first + drop), 128 * last
    for c in range(CHANS):
        row = jnp.broadcast_to(misfit[c : c + 1, 128 * first : end], (16, end - 128 * first)).astype(BF16)
        near = pltpu.roll(row, 1, 1, stride=1, stride_axis=0)
        far = pltpu.roll(near, 16, 1)
        at = 32 * (c % 4)
        shifted[c // 4, at : at + 16, begin:end] = near[:, 128 * drop :]
        shifted[c // 4, at + 16 : at + 32, begin:end] = far[:, 128 * drop :]


def correlate(shifted, gradient, spread, begin, end, pairs=(0, 1), add=False):
    def window_of(pair):
        return [
            shifted[cg, :, begin + 128 * h : end + 128 * h]
            for cg in range(4)
            for h in (2 * pair, 2 * pair + 1)
        ]

    multiply(gradient, window_of, spread, begin, end, pairs, add)


def gather_taps(spread, begin):
    total = spread[192:256, begin + 128 : begin + 640]
    for q in range(3):
        rows = spread[64 * q : 64 * q + 64, begin : begin + 640]
        total = total + pltpu.roll(rows, 96 - 32 * q, 1)[:, 128:]
    return total


def encode(value, scale):
    scaled = value * scale
    return (scaled * scaled * scaled * jnp.abs(scaled)).astype(BF16)


def decode(code, scale):
    power = code.astype(F32)
    root = jnp.sqrt(jnp.sqrt(jnp.abs(power))) * (1.0 / scale)
    return jnp.where(power < 0.0, -root, root)


def column_of(row):
    diagonal = tile_iota(ATOMS, ATOMS, 0) == tile_iota(ATOMS, ATOMS, 1)
    return jnp.sum(jnp.where(diagonal, jnp.broadcast_to(row, (ATOMS, ATOMS)), 0.0), axis=1, keepdims=True)


def kernel(
    slabs,
    bank_hbm,
    codes_hbm,
    signal_hbm,
    step_size_hbm,
    threshold_hbm,
    out_codes,
    out_residual,
    bank,
    codes,
    signal_in,
    step_size,
    threshold,
    natural,
    synthesis,
    gradient,
    lowered,
    own,
    code_shift,
    spread,
    part,
    coded_part,
    from_atom,
    atom_tail,
    from_next,
    from_before,
    misfit,
    misfit_shift,
    grad_send,
    grad_recv,
    code_send,
    scales,
    part_send,
    part_recv,
    grad_send_sem,
    grad_recv_sem,
    code_send_sem,
    code_recv_sem,
    load_sems,
    word,
):
    tm, atom, me = lax.axis_index("tm"), lax.axis_index("atom"), lax.axis_index("chan")
    after, before = lax.rem(tm + 1, slabs), lax.rem(tm + slabs - 1, slabs)
    other = 1 - atom
    has_before, has_after = tm > 0, tm < slabs - 1
    ends = has_before.astype(jnp.int32) + has_after.astype(jnp.int32)
    my_rows = pl.multiple_of(me // 4 * 16, 16)
    my_block = lax.rem(me, 4)

    def at_step(step):
        y, x, core = step
        return (
            lax.rem(me // 4 + y, 4) * 4 + lax.rem(me // 2 + x, 2) * 2 + lax.rem(me + core, 2)
        )

    def slot(step):
        return step[0] * 4 + step[1] * 2 + step[2]

    barrier = pltpu.get_barrier_semaphore()

    def signal(semaphore, device):
        pl.semaphore_signal(semaphore, 1, device_id=device, device_id_type=MESH)

    def signal_group(semaphore):
        for step in ((0, 0, 1), (0, 1, 0), (1, 0, 0), (2, 0, 0), (3, 0, 0)):
            signal(semaphore, {"chan": at_step(step)})

    for present, slab in ((has_after, after), (has_before, before)):

        @pl.when(present)
        def _(slab=slab):
            signal(barrier, {"tm": slab, "atom": other})
            signal(barrier, {"tm": slab})

    signal_group(barrier)
    signal(barrier, {"atom": other})
    loads = [
        pltpu.make_async_copy(source, target, load_sems.at[index])
        for index, (source, target) in enumerate(
            (
                (codes_hbm, codes),
                (bank_hbm, bank),
                (signal_hbm, signal_in),
                (step_size_hbm, step_size),
                (threshold_hbm, threshold),
            )
        )
    ]
    for load in loads:
        load.start()

    @pl.when(jnp.logical_not(has_before))
    def _():
        from_before[...] = jnp.zeros_like(from_before)

    @pl.when(jnp.logical_not(has_after))
    def _():
        from_next[...] = jnp.zeros_like(from_next)

    loads[0].wait()
    for block in range(8):
        lowered[block // 4, block % 4] = codes[:, 128 * block : 128 * block + 128].astype(BF16)
    for load in loads[1:]:
        load.wait()
    arrange_bank(bank, natural, synthesis, gradient)
    scales[:, 0:1] = column_of(step_size[...])
    scales[:, 1:2] = column_of(threshold[...])
    for half in range(2):
        at = pl.multiple_of((my_block + 4 * half) * 128, 128)
        own[half] = codes[pl.ds(my_rows, 16), pl.ds(at, 128)]

    code_shift[:, :, 256:384] = jnp.zeros((8, ATOMS, LANES), BF16)
    code_shift[:, :, 1536:] = jnp.zeros((8, ATOMS, LANES), BF16)
    spread[:, 1536:] = jnp.zeros((256, LANES), F32)
    pl.semaphore_wait(barrier, 6 + 2 * ends)
    signal_group(word.at[0])

    nothing = jnp.zeros((ATOMS, LANES), BF16)

    def codes_of(first, last):
        return [lowered[b // 4, b % 4] for b in range(first, last)]

    def keep_part(sweep, which, recon):
        if which < 2:
            own_signal = signal_in[:, HALF * which : HALF * which + HALF].astype(F32)
            recon = recon - jnp.where(atom == 0, own_signal, 0.0)
        if which < 2:
            part[sweep, which] = recon
        if which != 1:
            coded_part[sweep, which // 2] = encode(recon, GRAD_SCALE)

    def early_half(sweep):
        shift_codes(jnp.concatenate([nothing, *codes_of(0, 4), nothing], axis=1), 640, code_shift, 384)
        synthesize(code_shift, synthesis, spread, 0, 256, (0,))
        synthesize(code_shift, synthesis, spread, 256, 512)
        synthesize(code_shift, synthesis, spread, 512, 640)
        keep_part(sweep, 0, gather_rows(spread, 0))

    def tail(sweep):
        shift_codes(jnp.concatenate([*codes_of(3, 8), nothing], axis=1), 640, code_shift, 896)
        synthesize(code_shift, synthesis, spread, 1024, 1280)
        synthesize(code_shift, synthesis, spread, 1280, 1536, (1,))
        keep_part(sweep, 2, gather_rows(spread, 1024))

    def late_half(sweep):
        synthesize(code_shift, synthesis, spread, 512, 768)
        synthesize(code_shift, synthesis, spread, 768, 1024)
        keep_part(sweep, 1, gather_rows(spread, 512))

    def part_copy(sweep, index, source, target, device):
        return pltpu.make_async_remote_copy(
            src_ref=source,
            dst_ref=target,
            send_sem=part_send.at[sweep, index],
            recv_sem=part_recv.at[sweep, index],
            device_id=device,
            device_id_type=MESH,
        )

    def grad_copy(half, step):
        owner = at_step(step)
        return pltpu.make_async_remote_copy(
            src_ref=grad_send.at[half, owner],
            dst_ref=grad_recv.at[half, slot(step)],
            send_sem=grad_send_sem.at[half],
            recv_sem=grad_recv_sem.at[half],
            device_id={"chan": owner},
            device_id_type=MESH,
        )

    def code_place(last, half):
        if last:
            at = pl.multiple_of((my_block + 4 * half) * 128, 128)
            return out_codes.at[pl.ds(my_rows, 16), pl.ds(at, 128)]
        return lowered.at[half, my_block, pl.ds(my_rows, 16)]

    def code_copy(last, half, step):
        return pltpu.make_async_remote_copy(
            src_ref=code_send.at[half],
            dst_ref=code_place(last, half),
            send_sem=code_send_sem.at[half],
            recv_sem=code_recv_sem.at[half],
            device_id={"chan": at_step(step)},
            device_id_type=MESH,
        )

    others = [step for step in STEPS if slot(step)]

    def wait_pieces(sem, first):
        pieces = grad_recv.at[0, first:]
        pltpu.make_async_copy(pieces, pieces, sem).wait()

    sent = []
    for sweep in range(ITERS):
        last = sweep == ITERS - 1
        copies = [
            part_copy(sweep, index, source, target, device)
            for index, (source, target, device) in enumerate(
                (
                    (coded_part.at[sweep, 0], from_next.at[sweep, 1], {"tm": before, "atom": other}),
                    (coded_part.at[sweep, 0], from_next.at[sweep, 0], {"tm": before}),
                    (part.at[sweep, 0], from_atom.at[sweep, 0], {"atom": other}),
                    (coded_part.at[sweep, 1], from_before.at[sweep, 1], {"tm": after, "atom": other}),
                    (coded_part.at[sweep, 1], from_before.at[sweep, 0], {"tm": after}),
                    (coded_part.at[sweep, 1], atom_tail.at[sweep], {"atom": other}),
                    (part.at[sweep, 1], from_atom.at[sweep, 1], {"atom": other}),
                )
            )
        ]

        def start(first, end):
            for index in range(first, end):
                if index < 2:
                    pl.when(has_before)(copies[index].start)
                elif index in (3, 4):
                    pl.when(has_after)(copies[index].start)
                else:
                    copies[index].start()

        if sweep:
            wait_pieces(code_recv_sem.at[0], 1)
        early_half(sweep)
        start(0, 3)
        if sweep:
            wait_pieces(code_recv_sem.at[1], 1)
        tail(sweep)
        start(3, 6)
        late_half(sweep)
        start(6, 7)
        sent.append(copies)
        if sweep == 0:
            pl.semaphore_wait(word.at[0], 5)
            signal_group(word.at[1])

        def both(one, two):
            return decode(one[...], GRAD_SCALE) + decode(two[...], GRAD_SCALE)

        pl.when(has_after)(copies[0].wait_recv)
        pl.when(has_after)(copies[1].wait_recv)
        copies[5].wait_recv()
        edge = both(from_next.at[sweep, 0], from_next.at[sweep, 1]) + both(
            coded_part.at[sweep, 1], atom_tail.at[sweep]
        )
        misfit[:, SLAB:] = jnp.where(has_after, edge, 0.0)
        copies[2].wait_recv()
        pl.when(has_before)(copies[3].wait_recv)
        pl.when(has_before)(copies[4].wait_recv)
        whole = (part[sweep, 0] + from_atom[sweep, 0]) + both(
            from_before.at[sweep, 0], from_before.at[sweep, 1]
        )
        misfit[:, :HALF] = whole
        if last:
            out_residual[:, :HALF] = whole
        shift_misfit(misfit, 0, 4, 0, misfit_shift)
        correlate(misfit_shift, gradient, spread, 0, 128)
        copies[6].wait_recv()
        whole = part[sweep, 1] + from_atom[sweep, 1]
        misfit[:, HALF:SLAB] = whole
        if last:
            out_residual[:, HALF:SLAB] = whole
        shift_misfit(misfit, 3, 8, 1, misfit_shift)
        correlate(misfit_shift, gradient, spread, 128, 384)
        correlate(misfit_shift, gradient, spread, 384, 640)

        def put(half):
            total = gather_taps(spread, HALF * half)
            if last:
                wait_pieces(grad_send_sem.at[half], 1)
            for owner in range(GROUP):
                row, block = owner // 4 * 16, owner % 4 * 128
                piece = total[row : row + 16, block : block + 128]
                grad_send[half, owner] = encode(piece, GRAD_SCALE)
            if sweep == 0 and half == 0:
                pl.semaphore_wait(word.at[1], 5)
            for step in others:
                grad_copy(half, step).start()

        put(0)
        shift_misfit(misfit, 7, 12, 1, misfit_shift)
        correlate(misfit_shift, gradient, spread, 640, 896)
        correlate(misfit_shift, gradient, spread, 896, 1152)
        put(1)

        for half in range(2):
            wait_pieces(grad_recv_sem.at[half], 1)
            total = decode(grad_send[half, me], GRAD_SCALE)
            for turn in range(1, GROUP):
                total = total + decode(grad_recv[half, turn], GRAD_SCALE)
            step = scales[pl.ds(my_rows, 16), 0:1]
            bound = step * scales[pl.ds(my_rows, 16), 1:2]
            moved = own[half] - step * total
            updated = moved - jnp.clip(moved, -bound, bound)
            own[half] = updated
            if last:
                wait_pieces(code_send_sem.at[half], 1)
            code_send[half] = encode(updated, CODE_SCALE) if last else updated.astype(BF16)
            for step in others:
                code_copy(last, half, step).start()
            code_place(last, half)[...] = code_send[half]
        if last:
            for half in range(2):
                wait_pieces(code_recv_sem.at[half], 1)
                wait_pieces(code_send_sem.at[half], 1)
                wait_pieces(grad_send_sem.at[half], 1)
            for copy in (copy for group in sent for copy in group[:2]):
                pl.when(has_before)(copy.wait_send)
            for copy in (copy for group in sent for copy in group[3:5]):
                pl.when(has_after)(copy.wait_send)
            for group in sent:
                for index in (2, 5, 6):
                    group[index].wait_send()


def write_out(coded, residual, out_codes, out_residual, plain, sems):
    copies = [pltpu.make_async_copy(residual, out_residual, sems.at[4])]
    copies[0].start()
    for part in range(4):
        rows = pl.ds(16 * part, 16)
        plain[rows, :] = decode(coded[rows, :], CODE_SCALE)
        copies.append(pltpu.make_async_copy(plain.at[rows], out_codes.at[rows], sems.at[part]))
        copies[-1].start()
    for copy in copies:
        copy.wait()


def body(signal, codes_init, atom_bank, step_size, threshold):
    vmem = pl.BlockSpec(memory_space=pltpu.VMEM)
    coded, residual = pl.pallas_call(
        functools.partial(kernel, lax.axis_size("tm")),
        out_shape=(
            jax.ShapeDtypeStruct((ATOMS, SLAB), BF16),
            jax.ShapeDtypeStruct((CHANS, SLAB), F32),
        ),
        in_specs=[pl.BlockSpec(memory_space=pltpu.HBM)] * 5,
        out_specs=(vmem, vmem),
        scratch_shapes=[
            pltpu.VMEM((ATOMS * CHANS, TAPS), BF16),
            pltpu.VMEM((ATOMS, SLAB), F32),
            pltpu.VMEM((CHANS, SLAB), BF16),
            pltpu.VMEM((1, ATOMS), F32),
            pltpu.VMEM((1, ATOMS), F32),
            pltpu.VMEM((256, 2048), BF16),
            pltpu.VMEM((256, 2048), BF16),
            pltpu.VMEM((256, 2048), BF16),
            pltpu.VMEM((2, 4, ATOMS, LANES), BF16),
            pltpu.VMEM((2, 16, LANES), F32),
            pltpu.VMEM((8, ATOMS, 1664), BF16),
            pltpu.VMEM((256, 1664), F32),
            pltpu.VMEM((ITERS, 2, CHANS, HALF), F32),
            pltpu.VMEM((ITERS, 2, CHANS, HALF), BF16),
            pltpu.VMEM((ITERS, 2, CHANS, HALF), F32),
            pltpu.VMEM((ITERS, CHANS, HALF), BF16),
            pltpu.VMEM((ITERS, 2, CHANS, HALF), BF16),
            pltpu.VMEM((ITERS, 2, CHANS, HALF), BF16),
            pltpu.VMEM((CHANS, 1536), F32),
            pltpu.VMEM((4, 128, 1536), BF16),
            pltpu.VMEM((2, GROUP, 16, LANES), BF16),
            pltpu.VMEM((2, GROUP, 16, LANES), BF16),
            pltpu.VMEM((2, 16, LANES), BF16),
            pltpu.VMEM((ATOMS, LANES), F32),
            pltpu.SemaphoreType.DMA((ITERS, 7)),
            pltpu.SemaphoreType.DMA((ITERS, 7)),
            pltpu.SemaphoreType.DMA((2,)),
            pltpu.SemaphoreType.DMA((2,)),
            pltpu.SemaphoreType.DMA((2,)),
            pltpu.SemaphoreType.DMA((2,)),
            pltpu.SemaphoreType.DMA((5,)),
            pltpu.SemaphoreType.REGULAR((2,)),
        ],
        compiler_params=pltpu.CompilerParams(
            collective_id=0, has_side_effects=True, vmem_limit_bytes=48 * 1024 * 1024
        ),
    )(
        *(
            pltpu.with_memory_space_constraint(value, pltpu.HBM)
            for value in (
                atom_bank.reshape(ATOMS * CHANS, TAPS),
                codes_init,
                signal,
                step_size.reshape(1, ATOMS),
                threshold.reshape(1, ATOMS),
            )
        )
    )
    return pl.pallas_call(
        write_out,
        out_shape=(
            jax.ShapeDtypeStruct((ATOMS, SLAB), F32),
            jax.ShapeDtypeStruct((CHANS, SLAB), F32),
        ),
        in_specs=[vmem] * 2,
        out_specs=[pl.BlockSpec(memory_space=pltpu.HBM)] * 2,
        scratch_shapes=[pltpu.VMEM((ATOMS, SLAB), F32), pltpu.SemaphoreType.DMA((5,))],
    )(
        pltpu.with_memory_space_constraint(coded, pltpu.VMEM),
        pltpu.with_memory_space_constraint(residual, pltpu.VMEM),
    )


def solution(mesh):
    placed = (P("chan", "tm"), P("atom", "tm"), P("atom", "chan", None), P("atom"), P("atom"))
    return jax.shard_map(
        body,
        mesh=mesh,
        in_specs=placed,
        out_specs=(P("atom", "tm"), P("chan", "tm")),
        check_vma=False,
    )
```
